128 devices in a mesh: cluster: 16 (over x, z), head: 8 (over y, core).
Axes of the slice: x: 4, y: 4, z: 4, core: 2. Of those that a mesh axis runs over, the one named last changes fastest.
Arguments:
- features: bfloat16 [16384, 1024], P(('cluster', 'head')), may hold values from -80 to 80
- grad_out: bfloat16 [16384, 1024], P(('cluster', 'head')), may hold values from -6 to 6
- w_qkv: bfloat16 [1024, 3072], replicated, may hold values from -0.1875 to 0.1875
- w_out: bfloat16 [1024, 1024], replicated, may hold values from -0.1875 to 0.1875
- kept_slot: int32 [128, 8], P('cluster'), may hold values from 0 to 55, as said below
- kept_count: int32 [128], P('cluster'), may hold values from 1 to 8, as said below
- fetch_slots: int32 [16, 16, 3], replicated, may hold values from 0 to 7, as said below
Outputs:
- attended: bfloat16 [16384, 1024], P(('cluster', 'head'))
- grad_features: bfloat16 [16384, 1024], P(('cluster', 'head'))
The draws below stay inside these ranges and needn't reach their ends.
Inputs may be any that keep to these rules, and one draw needn't show every extreme that they name: fetch_slots[c, o] names 3 distinct blocks of cluster o, numbered 0 to 7 within o, that cluster c reads; every pair has exactly 3; the row o = c is never read. `kept_slot`: a position in the table of query block b's cluster c: below 8 the block of c of that number, else position 8 + o * 3 + r stands for fetch_slots[c, o, r], with o never c; entry 0 is the query block's own block; the entries of a row are distinct. `kept_count`: some query block keeps all 8 entries; clusters differ in how many they keep.
All inputs are finite; a program needn't handle non-finite values.
Results may differ from the reference program's by a relative error of at most 0.024.
The reference program's roundings to bfloat16 on the way count: a program that leaves them out, or rounds other values in their place, can miss the bound.
Values may be sent and summed in bfloat16 or wider, within the bound.
A program may use at most 128 MiB of HBM per device.

```python
import math
import jax
import jax.numpy as jnp
from jax import lax

HEADS = 16
HD = 64
D = 1024
BLK = 128
BLOCKS_CL = 8
KEPT = 8
SLOT = 3
NODES = 16384
N_CLUSTER = 16


def draw_features(key, part):
    key = jax.random.fold_in(key, 5)
    base_key = jax.random.fold_in(key, 0)
    values = jnp.clip(jax.random.normal(base_key, (NODES, D), jnp.float32), -6.0, 6.0)
    return values.astype(jnp.bfloat16)


def draw_fetch_slots(key, part):
    key = jax.random.fold_in(key, 7)
    keys_all = jax.random.split(key, N_CLUSTER * N_CLUSTER)
    orders = jax.vmap(lambda single: jax.random.permutation(single, BLOCKS_CL))(keys_all)
    return orders[:, :SLOT].reshape(N_CLUSTER, N_CLUSTER, SLOT).astype(jnp.int32)


def draw_kept_slot(key, part):
    key = jax.random.fold_in(key, 11)
    table_size = BLOCKS_CL + N_CLUSTER * SLOT
    block_count = BLOCKS_CL * N_CLUSTER
    keys_all = jax.random.split(key, block_count)
    ranks = jax.vmap(lambda single: jax.random.permutation(single, table_size))(keys_all).astype(jnp.int32)
    block_rows = jnp.arange(block_count, dtype=jnp.int32)[:, None]
    home = block_rows // BLOCKS_CL
    own_slot = block_rows % BLOCKS_CL
    positions = jnp.arange(table_size, dtype=jnp.int32)[None, :]
    source = (positions - BLOCKS_CL) // SLOT
    barred = (positions >= BLOCKS_CL) & (source == home)
    forced = (block_rows == 0) & (positions == table_size - 1)
    ranks = jnp.where(positions == own_slot, table_size + 1, jnp.where(forced, table_size, jnp.where(barred, -1 - positions, ranks)))
    return lax.top_k(ranks, KEPT)[1].astype(jnp.int32)


def draw_kept_count(key, part):
    key = jax.random.fold_in(key, 13)
    upper_key, level_key, peak_key = jax.random.split(key, 3)
    block_count = BLOCKS_CL * N_CLUSTER
    upper = jax.random.randint(upper_key, (N_CLUSTER,), KEPT // 4 + 1, KEPT + 1)
    upper = jnp.repeat(upper, BLOCKS_CL)
    levels = jax.random.randint(level_key, (block_count,), 0, 1 << 20)
    counts = 1 + levels % upper
    peak = jax.random.randint(peak_key, (), 0, block_count)
    return jnp.where(jnp.arange(block_count) == peak, KEPT, counts).astype(jnp.int32)


def steps_of(rng, dims, shards, smallest, high):
    factor_of = 1.0
    for axis_at, blocks in shards:
        draws = jax.random.uniform(jax.random.fold_in(jax.random.fold_in(rng, 6), axis_at), (blocks,), jnp.float32, smallest / len(shards), high / len(shards))
        factor_of = factor_of * jnp.repeat(jnp.exp(draws), dims[axis_at] // blocks).reshape((-1,) + (1,) * (len(dims) - 1 - axis_at))
    return factor_of


def centred(rng, extent, width, most, cuts=(), kind=jnp.bfloat16):
    array = width * jax.random.normal(rng, extent, jnp.float32)
    if cuts:
        array = array * steps_of(rng, extent, cuts, -0.22, 0.18)
    return jnp.clip(array, -most, most).astype(kind)


def setup_inputs(seed: int = 0) -> dict:
    streams_of = jax.random.split(jax.random.key(seed), 8)
    return {
        "features": draw_features(jax.random.fold_in(streams_of[7], 71), 0),
        "grad_out": centred(streams_of[1], (NODES, D), 1.0, 6.0, ((0, 128),)),
        "w_qkv": centred(streams_of[2], (D, 3 * D), D ** -0.5, 0.1875),
        "w_out": centred(streams_of[3], (D, D), D ** -0.5, 0.1875),
        "kept_slot": draw_kept_slot(jax.random.fold_in(streams_of[7], 71), 0),
        "kept_count": draw_kept_count(jax.random.fold_in(streams_of[7], 71), 0),
        "fetch_slots": draw_fetch_slots(jax.random.fold_in(streams_of[7], 71), 0),
    }


def global_ids(kept_slot, fetch_slots):
    block_rows = jnp.arange(kept_slot.shape[0], dtype=jnp.int32)[:, None]
    owner_here = block_rows // BLOCKS_CL
    fetched = jnp.maximum(kept_slot - BLOCKS_CL, 0)
    source = fetched // SLOT
    within = fetched % SLOT
    remote = fetch_slots[owner_here, source, within]
    return jnp.where(kept_slot < BLOCKS_CL, owner_here * BLOCKS_CL + kept_slot, source * BLOCKS_CL + remote).astype(jnp.int32)

def attention_weights(query_block, key_pick, live_mask):
    score_scale = 1.0 / math.sqrt(HD)
    scores = jnp.einsum('qhd,jkhd->hqjk', query_block.astype(jnp.float32), key_pick.astype(jnp.float32)) * score_scale
    scores = jnp.where(live_mask[None, None, :, None], scores, -jnp.inf)
    top_score = lax.optimization_barrier(jnp.max(scores, axis=(2, 3), keepdims=True))
    raised = jnp.exp(scores - top_score)
    return raised / lax.optimization_barrier(jnp.sum(raised, axis=(2, 3), keepdims=True))

def reference(features, grad_out, w_qkv, w_out, kept_slot, kept_count, fetch_slots):
    nblocks = kept_slot.shape[0]
    model_width = features.shape[1]
    total_rows = nblocks * BLK
    score_scale = 1.0 / math.sqrt(HD)
    qkv_rows = jnp.dot(features, w_qkv, preferred_element_type=jnp.float32).astype(jnp.bfloat16)
    grad_attn = lax.dot_general(grad_out, w_out, (((1,), (1,)), ((), ())), preferred_element_type=jnp.float32).astype(jnp.bfloat16)
    queries = qkv_rows[:, :model_width].reshape(nblocks, BLK, HEADS, HD)
    key_rows = qkv_rows[:, model_width:2 * model_width].reshape(nblocks, BLK, HEADS, HD)
    value_rows = qkv_rows[:, 2 * model_width:].reshape(nblocks, BLK, HEADS, HD)
    grad_blocks = grad_attn.reshape(nblocks, BLK, HEADS, HD)
    block_ids = global_ids(kept_slot, fetch_slots)
    live_all = jnp.arange(KEPT, dtype=jnp.int32)[None, :] < kept_count[:, None]

    def forward_block(items):
        query_block, picks, live_mask = items
        attention = attention_weights(query_block, key_rows[picks], live_mask)
        attention_low = lax.optimization_barrier(attention.astype(jnp.bfloat16)).astype(jnp.float32)
        return jnp.einsum('hqjk,jkhd->qhd', attention_low, value_rows[picks].astype(jnp.float32)).astype(jnp.bfloat16)
    attended_blocks = lax.map(forward_block, (queries, block_ids, live_all))

    def backward_block(carry, items):
        key_grads, value_grads = carry
        query_block, picks, live_mask, out_block, grad_block = items
        key_pick = key_rows[picks].astype(jnp.float32)
        value_pick = value_rows[picks].astype(jnp.float32)
        attention = attention_weights(query_block, key_rows[picks], live_mask)
        attention_low = lax.optimization_barrier(attention.astype(jnp.bfloat16)).astype(jnp.float32)
        grad_wide = grad_block.astype(jnp.float32)
        query_wide = query_block.astype(jnp.float32)
        grad_probs = jnp.einsum('qhd,jkhd->hqjk', grad_wide, value_pick)
        row_delta = lax.optimization_barrier(jnp.sum(grad_wide * out_block.astype(jnp.float32), axis=-1)).T
        grad_scores = attention * (grad_probs - row_delta[:, :, None, None]) * score_scale
        grad_scores = lax.optimization_barrier(grad_scores.astype(jnp.bfloat16)).astype(jnp.float32)
        grad_query = jnp.einsum('hqjk,jkhd->qhd', grad_scores, key_pick).astype(jnp.bfloat16)
        key_grads = key_grads.at[picks].add(jnp.einsum('hqjk,qhd->jkhd', grad_scores, query_wide))
        value_grads = value_grads.at[picks].add(jnp.einsum('hqjk,qhd->jkhd', attention_low, grad_wide))
        return ((key_grads, value_grads), grad_query)
    empty = jnp.zeros((nblocks, BLK, HEADS, HD), jnp.float32)
    (key_grads, value_grads), grad_queries = lax.scan(backward_block, (empty, empty), (queries, block_ids, live_all, attended_blocks, grad_blocks))
    grad_qkv = jnp.concatenate([grad_queries.reshape(total_rows, model_width), key_grads.astype(jnp.bfloat16).reshape(total_rows, model_width), value_grads.astype(jnp.bfloat16).reshape(total_rows, model_width)], axis=1)
    grad_features = lax.dot_general(grad_qkv, w_qkv, (((1,), (1,)), ((), ())), preferred_element_type=jnp.float32).astype(jnp.bfloat16)
    attended = jnp.dot(attended_blocks.reshape(total_rows, model_width), w_out, preferred_element_type=jnp.float32).astype(jnp.bfloat16)
    return (attended, grad_features)
```

```python
import functools

import jax
import jax.numpy as jnp
from jax import lax
from jax.experimental import pallas as pl
from jax.experimental.pallas import tpu as pltpu
from jax.sharding import PartitionSpec as P

MESH = pl.DeviceIdType.MESH
BF = jnp.bfloat16
F32 = jnp.float32
BLK = 128
NB = 8
SIDE = 4
SLOT = 3
FAR = (1, 3, 2)
VMEM_LIMIT = 56 << 20

NN = (((1,), (0,)), ((), ()))
NT = (((1,), (1,)), ((), ()))


def dot(a, b, dims=NN):
    return lax.dot_general(a, b, dims, preferred_element_type=F32)


def place():
    c = lax.axis_index("cluster")
    h = lax.axis_index("head")
    return c // SIDE, c % SIDE, h


def greet(x, z, h):
    barrier = pltpu.get_barrier_semaphore()
    for d in (1, 2, 3):
        pl.semaphore_signal(
            barrier, inc=1, device_id=(lax.rem(x + d, SIDE) * SIDE + z, h), device_id_type=MESH
        )
        pl.semaphore_signal(
            barrier, inc=1, device_id=(x * SIDE + lax.rem(z + d, SIDE), h), device_id_type=MESH
        )
    for d in range(1, NB):
        pl.semaphore_signal(
            barrier, inc=1, device_id=(x * SIDE + z, lax.rem(h + d, NB)), device_id_type=MESH
        )
    pl.semaphore_wait(barrier, 6 + NB - 1)


def forward_kernel(
    feat, gout, wqkv, wout, fetch,
    q_all, g_all, gk0, gk1, gk2, gk3, tk1, tk2, tk3, gv0, gv1, gv2, gv3, tv1, tv2, tv3,
    wk_v, wv_v, wq_v, wo_v, sendbuf, stage_k, stage_v,
    w_sem, y_send, y_recv, k_send, k_recv, v_send, v_recv, k2_send, k2_recv, v2_send, v2_recv,
):
    x, z, h = place()
    cluster = x * SIDE + z
    gk = (gk0, gk1, gk2, gk3)
    gv = (gv0, gv1, gv2, gv3)
    tk = (None, tk1, tk2, tk3)
    tv = (None, tv1, tv2, tv3)
    loads = [
        pltpu.make_async_copy(wqkv.at[:, pl.ds(1024, 1024)], wk_v, w_sem.at[0]),
        pltpu.make_async_copy(wqkv.at[:, pl.ds(2048, 1024)], wv_v, w_sem.at[1]),
        pltpu.make_async_copy(wqkv.at[:, pl.ds(0, 1024)], wq_v, w_sem.at[2]),
        pltpu.make_async_copy(wout, wo_v, w_sem.at[3]),
    ]
    for load in loads:
        load.start()
    greet(x, z, h)

    def project(part, rows, weight, dims, own):
        for p in range(4):
            if dims is NN:
                w = weight[:, p * 256 : (p + 1) * 256]
            else:
                w = weight[p * 256 : (p + 1) * 256, :]
            out = dot(rows[...], w, dims).astype(BF)
            sendbuf[part, 2 * p] = out[:, :128]
            sendbuf[part, 2 * p + 1] = out[:, 128:]
        own[h] = sendbuf[part, h]

    def y_copies(part, own):
        copies = []
        for d in range(1, NB):
            to = lax.rem(h + d, NB)
            copies.append(
                pltpu.make_async_remote_copy(
                    sendbuf.at[part, to], own.at[h], y_send.at[part, d - 1], y_recv.at[part, d - 1],
                    device_id=(cluster, to), device_id_type=MESH,
                )
            )
        return copies

    def recv_y(part, own):
        for d in range(1, NB):
            frm = lax.rem(h - d + NB, NB)
            pltpu.make_async_remote_copy(
                sendbuf.at[part, frm], own.at[frm], y_send.at[part, d - 1], y_recv.at[part, d - 1],
                device_id=(cluster, frm), device_id_type=MESH,
            ).wait_recv()

    loads[0].wait()
    project(0, feat, wk_v, NN, gk0)
    ycopy_k = y_copies(0, gk0)
    for copy in ycopy_k:
        copy.start()
    loads[1].wait()
    project(1, feat, wv_v, NN, gv0)
    ycopy_v = y_copies(1, gv0)
    for copy in ycopy_v:
        copy.start()
    loads[2].wait()
    project(2, feat, wq_v, NN, q_all)
    loads[3].wait()
    project(3, gout, wo_v, NT, g_all)

    def x_dev(d):
        return (lax.rem(x - d + SIDE, SIDE) * SIDE + z, h)

    def z_dev(d):
        return (x * SIDE + lax.rem(z - d + SIDE, SIDE), h)

    def first(own, dests, dev, send, recv):
        copies = {}
        for d in FAR:
            copies[d] = pltpu.make_async_remote_copy(
                own, dests[d], send.at[d - 1], recv.at[d - 1], device_id=dev(d), device_id_type=MESH
            )
            copies[d].start()
        return copies

    def second_k(e):
        copies = []
        source = lax.rem(x + e, SIDE) * SIDE + z
        for d in FAR:
            reader = x * SIDE + lax.rem(z - d + SIDE, SIDE)
            for r in range(SLOT):
                stage_k[d - 1, e, r] = gk[e][fetch[reader, source, r]]
            copy = pltpu.make_async_remote_copy(
                stage_k.at[d - 1, e], tk[d].at[e], k2_send.at[d - 1, e], k2_recv.at[d - 1, e],
                device_id=z_dev(d), device_id_type=MESH,
            )
            copy.start()
            copies.append(copy)
        return copies

    def second_v(e):
        copies = []
        source = x * SIDE + lax.rem(z + e, SIDE)
        for d in FAR:
            reader = lax.rem(x - d + SIDE, SIDE) * SIDE + z
            for r in range(SLOT):
                stage_v[d - 1, e, r] = gv[e][fetch[reader, source, r]]
            copy = pltpu.make_async_remote_copy(
                stage_v.at[d - 1, e], tv[d].at[e], v2_send.at[d - 1, e], v2_recv.at[d - 1, e],
                device_id=x_dev(d), device_id_type=MESH,
            )
            copy.start()
            copies.append(copy)
        return copies

    recv_y(0, gk0)
    copies_k = first(gk0, gk, x_dev, k_send, k_recv)
    seconds = second_k(0)
    recv_y(1, gv0)
    copies_v = first(gv0, gv, z_dev, v_send, v_recv)
    seconds += second_v(0)
    ycopy_q = y_copies(2, q_all)
    ycopy_g = y_copies(3, g_all)
    for copy in ycopy_q + ycopy_g:
        copy.start()
    for e in FAR:
        copies_k[e].wait_recv()
        seconds += second_k(e)
        copies_v[e].wait_recv()
        seconds += second_v(e)
    recv_y(2, q_all)
    recv_y(3, g_all)
    for copy in ycopy_k + ycopy_v + ycopy_q + ycopy_g:
        copy.wait_send()
    for d in FAR:
        copies_k[d].wait_send()
        copies_v[d].wait_send()
    for copy in seconds:
        copy.wait()


def attention_kernel(
    kept, count, fetch, q_all, g_all,
    gk0, gk1, gk2, gk3, tk1, tk2, tk3, gv0, gv1, gv2, gv3, tv1, tv2, tv3,
    attn_out, dq_out, dkg, dkt, dvg, dvt,
    kt, vt, dk, dv, sem,
):
    x, z, h = place()
    cluster = x * SIDE + z
    copies = []
    for n, (table, parts) in enumerate(
        ((kt, (gk0, gk1, gk2, gk3, tk1, tk2, tk3)), (vt, (gv0, gv1, gv2, gv3, tv1, tv2, tv3)))
    ):
        at = 0
        for m, part in enumerate(parts):
            rows = part.shape[0]
            copies.append(
                pltpu.make_async_copy(part, table.at[pl.ds(at, rows)], sem.at[n, m])
            )
            at += rows
    for copy in copies:
        copy.start()

    def clear(i, _):
        dk[i] = jnp.zeros((BLK, BLK), F32)
        dv[i] = jnp.zeros((BLK, BLK), F32)
        return 0

    lax.fori_loop(0, 68, clear, 0)
    for copy in copies:
        copy.wait()
    lane = lax.broadcasted_iota(jnp.int32, (BLK, BLK), 1)
    low = lane < 64

    def block(b, _):
        n = count[b]
        k_at, v_at = [], []
        for j in range(NB):
            t = jnp.where(j < n, kept[b, j], b)
            s = jnp.maximum(t - NB, 0)
            o = s // SLOT
            r = s - o * SLOT
            e = lax.rem(o // SIDE - x + SIDE, SIDE)
            f = lax.rem(o % SIDE - z + SIDE, SIDE)
            blk = fetch[cluster, o, r]
            k_far = jnp.where(f == 0, e * NB + blk, 32 + (f - 1) * 12 + e * SLOT + r)
            v_far = jnp.where(e == 0, f * NB + blk, 32 + (e - 1) * 12 + f * SLOT + r)
            k_at.append(jnp.where(t < NB, t, k_far))
            v_at.append(jnp.where(t < NB, t, v_far))
        kc = jnp.concatenate([kt[i] for i in k_at], axis=0)
        vc = jnp.concatenate([vt[i] for i in v_at], axis=0)
        q = q_all[b].astype(F32) * 0.125
        g = g_all[b].astype(F32)
        q_t = q.T.astype(BF)
        g_t = g.T.astype(BF)
        zero = jnp.zeros_like(q)
        probs, lows, outs = [], [], []
        for hh in range(2):
            mine = low if hh == 0 else jnp.logical_not(low)
            qh = jnp.where(mine, q, zero).astype(BF)
            s = dot(qh, kc, NT)
            s = jnp.concatenate(
                [jnp.where(j < n, s[:, j * BLK : (j + 1) * BLK], -jnp.inf) for j in range(NB)],
                axis=1,
            )
            p = jnp.exp(s - jnp.max(s, axis=1, keepdims=True))
            a = p * (1.0 / jnp.sum(p, axis=1, keepdims=True))
            al = a.astype(BF)
            probs.append(a)
            lows.append(al)
            outs.append(dot(al, vc))
        attn = jnp.where(low, outs[0], outs[1]).astype(BF)
        attn_out[b] = attn
        prod = g * attn.astype(F32)
        dqs = []
        for hh in range(2):
            mine = low if hh == 0 else jnp.logical_not(low)
            delta = jnp.sum(jnp.where(mine, prod, zero), axis=1, keepdims=True)
            gh = jnp.where(mine, g, zero).astype(BF)
            ds = (probs[hh] * (dot(gh, vc, NT) - delta)).astype(BF)
            dqs.append(dot(ds, kc))
            half = slice(hh * 64, (hh + 1) * 64)
            dk_t = dot(q_t[half], ds)
            dv_t = dot(g_t[half], lows[hh])
            for j in range(NB):
                cols = slice(j * BLK, (j + 1) * BLK)
                dk[k_at[j], half, :] += dk_t[:, cols]
                dv[v_at[j], half, :] += dv_t[:, cols]
        dq_out[b] = (jnp.where(low, dqs[0], dqs[1]) * 0.125).astype(BF)
        return 0

    lax.fori_loop(0, NB, block, 0)

    def flush_g(i, _):
        dkg[i] = dk[i]
        dvg[i] = dv[i]
        return 0

    def flush_t(i, _):
        dkt[i] = dk[i + 32].astype(BF)
        dvt[i] = dv[i + 32].astype(BF)
        return 0

    lax.fori_loop(0, 32, flush_g, 0)
    lax.fori_loop(0, 36, flush_t, 0)


def backward_kernel(
    fetch, attn, dq, dkg, dkt, dvg, dvt, wqkv, wout,
    attended, grad_features,
    rk0, rk1, rk2, rk3, rv0, rv1, rv2, rv3, sum_k, sum_v, back_k, back_v, own_k, own_v,
    attn_all, dq_all, dk_all, dv_all, wk_v, wv_v, wq_v, wo_v,
    w_sem, y_send, y_recv, k_send, k_recv, v_send, v_recv, k2_send, k2_recv, v2_send, v2_recv,
):
    x, z, h = place()
    cluster = x * SIDE + z
    rk = (rk0, rk1, rk2, rk3)
    rv = (rv0, rv1, rv2, rv3)
    loads = [
        pltpu.make_async_copy(wout, wo_v, w_sem.at[3]),
        pltpu.make_async_copy(wqkv.at[:, pl.ds(0, 1024)], wq_v, w_sem.at[2]),
        pltpu.make_async_copy(wqkv.at[:, pl.ds(1024, 1024)], wk_v, w_sem.at[0]),
        pltpu.make_async_copy(wqkv.at[:, pl.ds(2048, 1024)], wv_v, w_sem.at[1]),
    ]
    for load in loads:
        load.start()
    for ref in rk + rv:
        ref[12] = jnp.zeros((BLK, BLK), BF)
    greet(x, z, h)

    def x_dev(d):
        return (lax.rem(x + d, SIDE) * SIDE + z, h)

    def z_dev(d):
        return (x * SIDE + lax.rem(z + d, SIDE), h)

    def chunk(src, dests, dev, e, d, send, recv):
        return pltpu.make_async_remote_copy(
            src.at[pl.ds(((d - 1) * SIDE + e) * SLOT, SLOT)],
            dests[e].at[pl.ds((d - 1) * SLOT, SLOT)],
            send.at[d - 1, e], recv.at[d - 1, e],
            device_id=dev(d), device_id_type=MESH,
        )

    order = (2, 1, 3, 0)
    firsts = {}
    for e in order:
        for d in FAR:
            ck = chunk(dkt, rk, z_dev, e, d, k_send, k_recv)
            cv = chunk(dvt, rv, x_dev, e, d, v_send, v_recv)
            ck.start()
            cv.start()
            firsts[e, d] = (ck, cv)

    def y_copies(part, src, dest):
        copies = []
        for d in range(1, NB):
            to = lax.rem(h + d, NB)
            copies.append(
                pltpu.make_async_remote_copy(
                    src.at[to], dest.at[h], y_send.at[part, d - 1], y_recv.at[part, d - 1],
                    device_id=(cluster, to), device_id_type=MESH,
                )
            )
        for copy in copies:
            copy.start()
        dest[h] = src[h]
        return copies

    def recv_y(part, src, dest):
        for d in range(1, NB):
            frm = lax.rem(h - d + NB, NB)
            pltpu.make_async_remote_copy(
                src.at[frm], dest.at[frm], y_send.at[part, d - 1], y_recv.at[part, d - 1],
                device_id=(cluster, frm), device_id_type=MESH,
            ).wait_recv()

    ycopies = y_copies(0, attn, attn_all) + y_copies(1, dq, dq_all)

    def gathered(ref):
        return jnp.concatenate([ref[i] for i in range(NB)], axis=1)

    recv_y(0, attn, attn_all)
    loads[0].wait()
    attended[...] = dot(gathered(attn_all), wo_v[...]).astype(BF)
    recv_y(1, dq, dq_all)
    loads[1].wait()
    grad = dot(gathered(dq_all), wq_v[...], NT)

    def where_is(reader, source, blk, d):
        at = jnp.int32(12)
        for r in range(SLOT):
            at = jnp.where(fetch[reader, source, r] == blk, (d - 1) * SLOT + r, at)
        return at

    def total(e, base, got, reader_of, source, out):
        def one(blk, _):
            acc = base[e * NB + blk]
            for d in (1, 2, 3):
                acc = acc + got[e][where_is(reader_of(d), source, blk, d)].astype(F32)
            out(blk, acc)
            return 0

        lax.fori_loop(0, NB, one, 0)

    backs = []
    for e in order:
        for d in FAR:
            firsts[e, d][0].wait_recv()

        def put_k(blk, acc, e=e):
            if e == 0:
                own_k[blk] = acc
            else:
                sum_k[e - 1, blk] = acc.astype(BF)

        total(
            e, dkg, rk, lambda d: x * SIDE + lax.rem(z - d + SIDE, SIDE),
            lax.rem(x + e, SIDE) * SIDE + z, put_k,
        )
        if e:
            copy = pltpu.make_async_remote_copy(
                sum_k.at[e - 1], back_k.at[e - 1], k2_send.at[e - 1], k2_recv.at[e - 1],
                device_id=x_dev(e), device_id_type=MESH,
            )
            copy.start()
            backs.append(copy)
        for d in FAR:
            firsts[e, d][1].wait_recv()

        def put_v(blk, acc, e=e):
            if e == 0:
                own_v[blk] = acc
            else:
                sum_v[e - 1, blk] = acc.astype(BF)

        total(
            e, dvg, rv, lambda d: lax.rem(x - d + SIDE, SIDE) * SIDE + z,
            x * SIDE + lax.rem(z + e, SIDE), put_v,
        )
        if e:
            copy = pltpu.make_async_remote_copy(
                sum_v.at[e - 1], back_v.at[e - 1], v2_send.at[e - 1], v2_recv.at[e - 1],
                device_id=z_dev(e), device_id_type=MESH,
            )
            copy.start()
            backs.append(copy)

    for copy in backs:
        copy.wait()

    def finish(own, back, out):
        def one(blk, _):
            acc = own[blk]
            for d in range(3):
                acc = acc + back[d, blk].astype(F32)
            out[blk] = acc.T.astype(BF)
            return 0

        lax.fori_loop(0, NB, one, 0)

    finish(own_k, back_k, sum_k.at[0])
    ycopies += y_copies(2, sum_k.at[0], dk_all)
    finish(own_v, back_v, sum_v.at[0])
    ycopies += y_copies(3, sum_v.at[0], dv_all)
    recv_y(2, sum_k.at[0], dk_all)
    loads[2].wait()
    grad = grad + dot(gathered(dk_all), wk_v[...], NT)
    recv_y(3, sum_v.at[0], dv_all)
    loads[3].wait()
    grad = grad + dot(gathered(dv_all), wv_v[...], NT)
    grad_features[...] = grad.astype(BF)
    for copy in ycopies:
        copy.wait_send()
    for pair in firsts.values():
        pair[0].wait_send()
        pair[1].wait_send()


def vmem():
    return pl.BlockSpec(memory_space=pltpu.VMEM)


def anym():
    return pl.BlockSpec(memory_space=pl.ANY)


def smem():
    return pl.BlockSpec(memory_space=pltpu.SMEM)


def shards(features, grad_out, w_qkv, w_out, kept_slot, kept_count, fetch_slots):
    dma = pltpu.SemaphoreType.DMA
    tile = (BLK, BLK)
    own = jax.ShapeDtypeStruct((NB,) + tile, BF)
    far = jax.ShapeDtypeStruct((SIDE, SLOT) + tile, BF)
    weights = [pltpu.VMEM((1024, 1024), BF) for _ in range(4)]
    moved = pl.pallas_call(
        forward_kernel,
        out_shape=[own, own] + ([own] * 4 + [far] * 3) * 2,
        in_specs=[vmem(), vmem(), anym(), anym(), smem()],
        out_specs=[vmem()] * 16,
        scratch_shapes=weights
        + [
            pltpu.VMEM((4, NB) + tile, BF),
            pltpu.VMEM((3, SIDE, SLOT) + tile, BF),
            pltpu.VMEM((3, SIDE, SLOT) + tile, BF),
            dma((4,)), dma((4, NB - 1)), dma((4, NB - 1)),
            dma((3,)), dma((3,)), dma((3,)), dma((3,)),
            dma((3, SIDE)), dma((3, SIDE)), dma((3, SIDE)), dma((3, SIDE)),
        ],
        compiler_params=pltpu.CompilerParams(
            collective_id=0, has_side_effects=True, vmem_limit_bytes=VMEM_LIMIT
        ),
    )(features, grad_out, w_qkv, w_out, fetch_slots)
    q_all, g_all = moved[:2]
    tables = [m.reshape((-1,) + tile) for m in moved[2:]]
    wide = jax.ShapeDtypeStruct((32,) + tile, F32)
    slim = jax.ShapeDtypeStruct((36,) + tile, BF)
    attn, dq, dkg, dkt, dvg, dvt = pl.pallas_call(
        attention_kernel,
        out_shape=[own, own, wide, slim, wide, slim],
        in_specs=[smem()] * 3 + [vmem()] * 2 + [anym()] * 14,
        out_specs=[vmem()] * 6,
        scratch_shapes=[
            pltpu.VMEM((68,) + tile, BF),
            pltpu.VMEM((68,) + tile, BF),
            pltpu.VMEM((68,) + tile, F32),
            pltpu.VMEM((68,) + tile, F32),
            dma((2, 7)),
        ],
        compiler_params=pltpu.CompilerParams(vmem_limit_bytes=VMEM_LIMIT),
    )(kept_slot, kept_count, fetch_slots, q_all, g_all, *tables)
    rows, width = features.shape
    got = [pltpu.VMEM((13,) + tile, BF) for _ in range(8)]
    return pl.pallas_call(
        backward_kernel,
        out_shape=[jax.ShapeDtypeStruct((rows, width), BF)] * 2,
        in_specs=[smem()] + [vmem()] * 6 + [anym()] * 2,
        out_specs=[vmem()] * 2,
        scratch_shapes=got
        + [pltpu.VMEM((3, NB) + tile, BF) for _ in range(4)]
        + [pltpu.VMEM((NB,) + tile, F32) for _ in range(2)]
        + [pltpu.VMEM((NB,) + tile, BF) for _ in range(4)]
        + weights
        + [
            dma((4,)), dma((4, NB - 1)), dma((4, NB - 1)),
            dma((3, SIDE)), dma((3, SIDE)), dma((3, SIDE)), dma((3, SIDE)),
            dma((3,)), dma((3,)), dma((3,)), dma((3,)),
        ],
        compiler_params=pltpu.CompilerParams(
            collective_id=1, has_side_effects=True, vmem_limit_bytes=VMEM_LIMIT
        ),
    )(fetch_slots, attn, dq, dkg, dkt, dvg, dvt, w_qkv, w_out)


def solution(mesh):
    rows = P(("cluster", "head"), None)
    in_specs = (rows, rows, P(), P(), P("cluster", None), P("cluster"), P())
    return jax.shard_map(
        shards, mesh=mesh, in_specs=in_specs, out_specs=(rows, rows), check_vma=False
    )
```

```python
import jax
import jax.numpy as jnp
from jax import lax
from jax.experimental import pallas as pl
from jax.experimental.pallas import tpu as pltpu
from jax.sharding import PartitionSpec as P

MESH = pl.DeviceIdType.MESH
BF = jnp.bfloat16
F32 = jnp.float32
BLK = 128
HD = 64
NB = 8
SIDE = 4
SLOT = 3
TABLE = NB + SIDE * SIDE * SLOT
LIVE = NB * NB
NEAR = (1, 3, 2)
OUTWARD = (2, 1, 3, 0)
VMEM_LIMIT = 56 << 20

NN = (((1,), (0,)), ((), ()))
NT = (((1,), (1,)), ((), ()))


def dot(a, b, dims=NN):
    return lax.dot_general(a, b, dims, preferred_element_type=F32)


def back_by(d):
    return (SIDE - d) % SIDE


def base(part, d, e):
    return NB + ((e * SIDE + d) if part == 0 else (d * SIDE + e)) * SLOT


def sublayer_kernel(refs):
    feat, gout, wqkv, wout = refs["feat"], refs["gout"], refs["wqkv"], refs["wout"]
    code, count, inverse, fetch = refs["code"], refs["count"], refs["inverse"], refs["fetch"]
    first, table, stage = refs["first"], refs["table"], refs["stage"]
    terms, slot_out, got = refs["terms"], refs["slot_out"], refs["got"]
    own_sum, back_out, back_in = refs["own_sum"], refs["back_out"], refs["back_in"]
    final = refs["final"]
    c = lax.axis_index("cluster")
    h = lax.axis_index("head")
    x, z = c // SIDE, c % SIDE

    def at(part, a, b):
        if part == 1:
            a, b = b, a
        return lax.rem(x + a, SIDE) * SIDE + lax.rem(z + b, SIDE)

    loads = []
    for n, piece in enumerate((1, 2, 0)):
        loads.append(
            pltpu.make_async_copy(
                wqkv.at[:, pl.ds(piece * 1024, 1024)], refs["w"][n], refs["w_sem"].at[n]
            )
        )
    loads.append(pltpu.make_async_copy(wout, refs["w"][3], refs["w_sem"].at[3]))
    for load in loads:
        load.start()

    barrier = pltpu.get_barrier_semaphore()
    for d in (1, 2, 3):
        for part in range(2):
            pl.semaphore_signal(
                barrier, inc=1, device_id=(at(part, d, 0), h), device_id_type=MESH
            )
    for d in range(1, NB):
        pl.semaphore_signal(
            barrier, inc=1, device_id=(c, lax.rem(h + d, NB)), device_id_type=MESH
        )

    pending = []

    def remote(src, dst, send, recv, device):
        return pltpu.make_async_remote_copy(
            src, dst, send, recv, device_id=device, device_id_type=MESH
        )

    def y_copy(kind, src, dst, peer, d):
        return remote(
            src, dst, refs["y_send"].at[kind, d - 1], refs["y_recv"].at[kind, d - 1], (c, peer)
        )

    def y_start(kind, src, dest):
        for d in range(1, NB):
            to = lax.rem(h + d, NB)
            y_copy(kind, src.at[to], dest.at[h], to, d).start()
            pending.append(lambda to=to, d=d: y_copy(kind, src.at[to], dest.at[h], to, d))
        dest[h] = src[h]

    def y_wait(kind, src, dest):
        for d in range(1, NB):
            frm = lax.rem(h - d + NB, NB)
            y_copy(kind, src.at[frm], dest.at[frm], frm, d).wait_recv()

    def project(rows, weight, dims, put):
        for p in range(4):
            if dims is NN:
                w = weight[:, p * 256 : (p + 1) * 256]
            else:
                w = weight[p * 256 : (p + 1) * 256, :]
            out = dot(rows[...], w, dims)
            put(2 * p, out[:, :BLK].T.astype(BF))
            put(2 * p + 1, out[:, BLK:].T.astype(BF))

    def put_heads(part):
        def put(dest, tile):
            refs["y_out"][part][0][dest] = tile[:HD]
            refs["y_out"][part][1][dest] = tile[HD:]

        return put

    def put_whole(n):
        def put(dest, tile):
            refs["qg_out"][n][dest] = tile

        return put

    loads[0].wait()
    project(feat, refs["w"][0], NN, put_heads(0))
    pl.semaphore_wait(barrier, 6 + NB - 1)
    y_start(0, refs["y_out"][0][0], first[0][0][0])
    loads[1].wait()
    project(feat, refs["w"][1], NN, put_heads(1))
    y_start(2, refs["y_out"][1][0], first[1][0][0])
    y_start(1, refs["y_out"][0][1], first[0][1][0])
    y_start(3, refs["y_out"][1][1], first[1][1][0])
    loads[2].wait()
    project(feat, refs["w"][2], NN, put_whole(0))
    y_start(4, refs["qg_out"][0], refs["qg"][0])
    loads[3].wait()
    project(gout, refs["w"][3], NT, put_whole(1))
    y_start(5, refs["qg_out"][1], refs["qg"][1])

    def spread_copy(hh, part, e):
        return remote(
            first[part][hh][0], first[part][hh][e],
            refs["f_send"].at[hh, part, e - 1], refs["f_recv"].at[hh, part, e - 1],
            (at(part, back_by(e), 0), h),
        )

    def pick_copy(hh, part, d, e):
        return remote(
            stage[part][hh].at[d - 1, e],
            table[part][hh].at[pl.ds(base(part, d, e), SLOT)],
            refs["s_send"].at[hh, part, d - 1, e], refs["s_recv"].at[hh, part, d - 1, e],
            (at(part, 0, back_by(d)), h),
        )

    def pick(hh, part, e):
        source = at(part, e, 0)
        for d in NEAR:
            reader = at(part, 0, back_by(d))
            for r in range(SLOT):
                stage[part][hh][d - 1, e, r] = first[part][hh][e][fetch[r, reader, source]]
            pick_copy(hh, part, d, e).start()
            pending.append(lambda d=d: pick_copy(hh, part, d, e))

    def keep(hh, part, e):
        if e == 0:
            for t in range(NB):
                table[part][hh][t] = first[part][hh][0][t]
        else:
            source = at(part, e, 0)
            for r in range(SLOT):
                table[part][hh][base(part, 0, e) + r] = first[part][hh][e][fetch[r, c, source]]

    def forward_start(hh):
        for part in range(2):
            y_wait(2 * part + hh, refs["y_out"][part][hh], first[part][hh][0])
            for e in NEAR:
                spread_copy(hh, part, e).start()
                pending.append(lambda part=part, e=e: spread_copy(hh, part, e))
            pick(hh, part, 0)
        for part in range(2):
            keep(hh, part, 0)

    def forward_step(hh, e):
        for part in range(2):
            spread_copy(hh, part, e).wait_recv()
            pick(hh, part, e)
            keep(hh, part, e)

    def forward_done(hh):
        for part in range(2):
            for e in range(SIDE):
                for d in NEAR:
                    pick_copy(hh, part, d, e).wait_recv()

    def attention(hh, hooks):
        half = slice(hh * HD, (hh + 1) * HD)

        def block(b, _):
            for when, hook in hooks.items():
                pl.when(b == when)(hook)
            n = count[b]
            slots = [code[b, j] for j in range(NB)]
            kc = jnp.concatenate([table[0][hh][i] for i in slots], axis=1)
            vc = jnp.concatenate([table[1][hh][i] for i in slots], axis=1)
            q_t = refs["qg"][0][b, half, :].astype(F32) * 0.125
            g_t = refs["qg"][1][b, half, :].astype(F32)
            q = q_t.T.astype(BF)
            g32 = g_t.T
            g = g32.astype(BF)
            s = dot(q, kc)
            s = jnp.concatenate(
                [jnp.where(j < n, s[:, j * BLK : (j + 1) * BLK], -jnp.inf) for j in range(NB)],
                axis=1,
            )
            p = jnp.exp(s - jnp.max(s, axis=1, keepdims=True))
            a = p * (1.0 / jnp.sum(p, axis=1, keepdims=True))
            low = a.astype(BF)
            attn = dot(low, vc, NT).astype(BF)
            delta = jnp.sum(g32 * attn.astype(F32), axis=1, keepdims=True)
            ds = (a * (dot(g, vc) - delta)).astype(BF)
            dq = (dot(ds, kc, NT) * 0.125).astype(BF)
            dk_t = dot(q_t.astype(BF), ds)
            dv_t = dot(g_t.astype(BF), low)
            for j in range(NB):
                cols = slice(j * BLK, (j + 1) * BLK)
                terms[0][b * NB + j] = dk_t[:, cols]
                terms[1][b * NB + j] = dv_t[:, cols]
            if hh == 0:
                refs["half"][0][b] = attn
                refs["half"][1][b] = dq
            else:
                refs["row_out"][0][b] = jnp.concatenate([refs["half"][0][b], attn], axis=1)
                refs["row_out"][1][b] = jnp.concatenate([refs["half"][1][b], dq], axis=1)
            return 0

        lax.fori_loop(0, NB, block, 0)

    def slot_total(part, slot):
        acc = terms[part][inverse[slot * NB]]
        for b in range(1, NB):
            acc = acc + terms[part][inverse[slot * NB + b]]
        return acc

    def slot_copy(hh, part, d, e):
        return remote(
            slot_out[part][hh].at[d - 1, e],
            got[part][hh][e].at[pl.ds((d - 1) * SLOT, SLOT)],
            refs["g_send"].at[hh, part, d - 1, e], refs["g_recv"].at[hh, part, d - 1, e],
            (at(part, 0, d), h),
        )

    def backward_start(hh):
        for e in OUTWARD:
            for d in NEAR:
                for part in range(2):

                    def one(r, _, e=e, d=d, part=part):
                        total = slot_total(part, base(part, d, e) + r)
                        slot_out[part][hh][d - 1, e, r] = total.astype(BF)
                        return 0

                    lax.fori_loop(0, SLOT, one, 0)
                    slot_copy(hh, part, d, e).start()
                    pending.append(lambda part=part, d=d, e=e: slot_copy(hh, part, d, e))
        for part in range(2):
            for e in (1, 2, 3):

                def near(r, _, e=e, part=part):
                    total = slot_total(part, base(part, 0, e) + r)
                    got[part][hh][e][9 + r] = total.astype(BF)
                    return 0

                lax.fori_loop(0, SLOT, near, 0)

            def own(t, _, part=part):
                own_sum[part][hh][t] = slot_total(part, t)
                return 0

            lax.fori_loop(0, NB, own, 0)

    def back_copy(hh, part, e):
        return remote(
            back_out[part][hh].at[e - 1], back_in[part][hh].at[e - 1],
            refs["b_send"].at[hh, part, e - 1], refs["b_recv"].at[hh, part, e - 1],
            (at(part, e, 0), h),
        )

    def backward_step(hh, e):
        for part in range(2):
            for d in NEAR:
                slot_copy(hh, part, d, e).wait_recv()
            source = at(part, e, 0)

            def one(t, _, part=part, source=source):
                acc = own_sum[part][hh][t] if e == 0 else None
                for d in (0, 1, 2, 3):
                    if d == 0 and e == 0:
                        continue
                    reader = at(part, 0, back_by(d))
                    place = 12
                    for r in range(SLOT):
                        here = (9 if d == 0 else (d - 1) * SLOT) + r
                        place = jnp.where(fetch[r, reader, source] == t, here, place)
                    term = got[part][hh][e][place].astype(F32)
                    acc = term if acc is None else acc + term
                if e == 0:
                    own_sum[part][hh][t] = acc
                else:
                    back_out[part][hh][e - 1, t] = acc.astype(BF)
                return 0

            lax.fori_loop(0, NB, one, 0)
            if e:
                back_copy(hh, part, e).start()
                pending.append(lambda part=part: back_copy(hh, part, e))

    def backward_finish(hh):
        for part in range(2):
            for e in (1, 2, 3):
                back_copy(hh, part, e).wait_recv()

            def one(t, _, part=part):
                acc = own_sum[part][hh][t]
                for e in range(3):
                    acc = acc + back_in[part][hh][e, t].astype(F32)
                final[part][hh][t] = acc.astype(BF)
                return 0

            lax.fori_loop(0, NB, one, 0)
            y_start(8 + 2 * part + hh, final[part][hh], refs["grads"][part][hh])

    forward_start(0)
    for e in NEAR:
        forward_step(0, e)
    forward_start(1)
    for part in range(2):
        terms[part][LIVE] = jnp.zeros((HD, BLK), F32)
        for hh in range(2):
            for e in range(SIDE):
                got[part][hh][e][12] = jnp.zeros((HD, BLK), BF)
    y_wait(4, refs["qg_out"][0], refs["qg"][0])
    y_wait(5, refs["qg_out"][1], refs["qg"][1])
    forward_done(0)
    attention(0, {n + 1: (lambda e=e: forward_step(1, e)) for n, e in enumerate(NEAR)})
    backward_start(0)
    forward_done(1)
    attention(1, {n + 2: (lambda e=e: backward_step(0, e)) for n, e in enumerate(OUTWARD)})
    backward_start(1)
    y_start(6, refs["row_out"][0], refs["rows"][0])
    y_start(7, refs["row_out"][1], refs["rows"][1])
    backward_finish(0)

    def wide(ref):
        return jnp.concatenate([ref[i] for i in range(NB)], axis=1)

    def wide_t(part):
        tiles = []
        for i in range(NB):
            tile = jnp.concatenate([refs["grads"][part][hh][i] for hh in range(2)], axis=0)
            tiles.append(tile.astype(F32).T.astype(BF))
        return jnp.concatenate(tiles, axis=1)

    y_wait(6, refs["row_out"][0], refs["rows"][0])
    refs["attended"][...] = dot(wide(refs["rows"][0]), refs["w"][3][...]).astype(BF)
    y_wait(7, refs["row_out"][1], refs["rows"][1])
    refs["grad"][...] = dot(wide(refs["rows"][1]), refs["w"][2][...], NT)
    for e in OUTWARD:
        backward_step(1, e)
    backward_finish(1)
    for part in range(2):
        for hh in range(2):
            y_wait(8 + 2 * part + hh, final[part][hh], refs["grads"][part][hh])
        term = dot(wide_t(part), refs["w"][part][...], NT)
        if part == 0:
            refs["grad"][...] += term
        else:
            refs["grad_features"][...] = (refs["grad"][...] + term).astype(BF)
    for copy in pending:
        copy().wait_send()


def tree_call(layout, kernel):
    flat, tree = jax.tree.flatten(layout, is_leaf=lambda leaf: not isinstance(leaf, (list, dict)))

    def called(names, *refs):
        kernel({**names, **jax.tree.unflatten(tree, refs)})

    return flat, called


def shards(features, grad_out, w_qkv, w_out, kept_slot, kept_count, fetch_slots):
    dma = pltpu.SemaphoreType.DMA
    c = lax.axis_index("cluster")
    x, z = c // SIDE, c % SIDE
    fetched = jnp.maximum(kept_slot - NB, 0)
    source = fetched // SLOT
    e = (source // SIDE - x + SIDE) % SIDE
    f = (source % SIDE - z + SIDE) % SIDE
    relative = NB + (e * SIDE + f) * SLOT + fetched % SLOT
    code = jnp.where(kept_slot < NB, kept_slot, relative)
    entry = jnp.arange(NB, dtype=jnp.int32)
    live = entry[None, :] < kept_count[:, None]
    code = jnp.where(live, code, entry[:, None])
    slots = jnp.arange(TABLE, dtype=jnp.int32)
    hits = (code[None] == slots[:, None, None]) & live[None]
    spot = entry[:, None] * NB + entry[None, :]
    inverse = jnp.min(jnp.where(hits, spot[None], LIVE), axis=2).reshape(-1)

    def vm(*shape, dtype=BF):
        return pltpu.VMEM(shape, dtype)

    def each(make, *counts):
        if not counts:
            return make()
        return [each(make, *counts[1:]) for _ in range(counts[0])]

    tile = (HD, BLK)
    layout = {
        "w": each(lambda: vm(1024, 1024), 4),
        "y_out": each(lambda: vm(NB, *tile), 2, 2),
        "qg_out": each(lambda: vm(NB, BLK, BLK), 2),
        "qg": each(lambda: vm(NB, BLK, BLK), 2),
        "first": each(lambda: vm(NB, *tile), 2, 2, SIDE),
        "table": each(lambda: vm(TABLE, *tile), 2, 2),
        "stage": each(lambda: vm(3, SIDE, SLOT, *tile), 2, 2),
        "terms": each(lambda: vm(LIVE + 1, *tile, dtype=F32), 2),
        "half": each(lambda: vm(NB, BLK, HD), 2),
        "row_out": each(lambda: vm(NB, BLK, BLK), 2),
        "rows": each(lambda: vm(NB, BLK, BLK), 2),
        "slot_out": each(lambda: vm(3, SIDE, SLOT, *tile), 2, 2),
        "got": each(lambda: vm(13, *tile), 2, 2, SIDE),
        "own_sum": each(lambda: vm(NB, *tile, dtype=F32), 2, 2),
        "back_out": each(lambda: vm(3, NB, *tile), 2, 2),
        "back_in": each(lambda: vm(3, NB, *tile), 2, 2),
        "final": each(lambda: vm(NB, *tile), 2, 2),
        "grads": each(lambda: vm(NB, *tile), 2, 2),
        "grad": vm(BLK, 1024, dtype=F32),
        "w_sem": dma((4,)),
        "y_send": dma((12, NB - 1)),
        "y_recv": dma((12, NB - 1)),
        "f_send": dma((2, 2, 3)),
        "f_recv": dma((2, 2, 3)),
        "s_send": dma((2, 2, 3, SIDE)),
        "s_recv": dma((2, 2, 3, SIDE)),
        "g_send": dma((2, 2, 3, SIDE)),
        "g_recv": dma((2, 2, 3, SIDE)),
        "b_send": dma((2, 2, 3)),
        "b_recv": dma((2, 2, 3)),
    }
    scratch, called = tree_call(layout, sublayer_kernel)
    names = ("feat", "gout", "wqkv", "wout", "code", "count", "inverse", "fetch")
    names += ("attended", "grad_features")

    def kernel(*refs):
        called(dict(zip(names, refs)), *refs[len(names) :])

    spec = pl.BlockSpec
    near = spec(memory_space=pltpu.VMEM)
    far = spec(memory_space=pl.ANY)
    scalars = spec(memory_space=pltpu.SMEM)
    return pl.pallas_call(
        kernel,
        out_shape=[jax.ShapeDtypeStruct(features.shape, BF)] * 2,
        in_specs=[near, near, far, far, scalars, scalars, scalars, scalars],
        out_specs=[near, near],
        scratch_shapes=scratch,
        compiler_params=pltpu.CompilerParams(
            collective_id=0, has_side_effects=True, vmem_limit_bytes=VMEM_LIMIT
        ),
    )(
        features, grad_out, w_qkv, w_out, code, kept_count, inverse,
        jnp.transpose(fetch_slots, (2, 0, 1)),
    )


def solution(mesh):
    rows = P(("cluster", "head"), None)
    in_specs = (rows, rows, P(), P(), P("cluster", None), P("cluster"), P())
    return jax.shard_map(
        shards, mesh=mesh, in_specs=in_specs, out_specs=(rows, rows), check_vma=False
    )
```

```python
import jax
import jax.numpy as jnp
from jax import lax
from jax.experimental import pallas as pl
from jax.experimental.pallas import tpu as pltpu
from jax.sharding import PartitionSpec as P

MESH = pl.DeviceIdType.MESH
BF = jnp.bfloat16
F32 = jnp.float32
BLK = 128
HD = 64
NB = 8
SIDE = 4
SLOT = 3
TABLE = NB + SIDE * SIDE * SLOT
LIVE = NB * NB
NEAR = (1, 3, 2)
OUTWARD = (2, 1, 3, 0)
VMEM_LIMIT = 56 << 20

NN = (((1,), (0,)), ((), ()))
NT = (((1,), (1,)), ((), ()))


def dot(a, b, dims=NN):
    return lax.dot_general(a, b, dims, preferred_element_type=F32)


def back_by(d):
    return (SIDE - d) % SIDE


def base(part, d, e):
    return NB + ((e * SIDE + d) if part == 0 else (d * SIDE + e)) * SLOT


def sublayer_kernel(refs):
    feat, gout, wqkv, wout = refs["feat"], refs["gout"], refs["wqkv"], refs["wout"]
    index, count, fetch = refs["index"], refs["count"], refs["fetch"]
    first, table, stage = refs["first"], refs["table"], refs["stage"]
    terms, slot_out, got = refs["terms"], refs["slot_out"], refs["got"]
    own_sum, back_out, back_in = refs["own_sum"], refs["back_out"], refs["back_in"]
    final = refs["final"]
    c = lax.axis_index("cluster")
    h = lax.axis_index("head")
    x, z = c // SIDE, c % SIDE

    def at(part, a, b):
        if part == 1:
            a, b = b, a
        return lax.rem(x + a, SIDE) * SIDE + lax.rem(z + b, SIDE)

    def load(n, src, dst):
        return pltpu.make_async_copy(src, dst, refs["w_sem"].at[n])

    loads = [load(4, refs["feat_in"], feat), load(5, refs["gout_in"], gout)]
    for n, piece in enumerate((1, 2, 0)):
        loads.append(load(n, wqkv.at[:, pl.ds(piece * 1024, 1024)], refs["w"][n]))
    loads.append(load(3, wout, refs["w"][3]))
    load_feat, load_gout, load_k, load_v, load_q, load_o = loads
    load_feat.start()
    load_k.start()
    load_v.start()

    barrier = pltpu.get_barrier_semaphore()
    for d in (1, 2, 3):
        for part in range(2):
            pl.semaphore_signal(
                barrier, inc=1, device_id=(at(part, d, 0), h), device_id_type=MESH
            )
    for d in range(1, NB):
        pl.semaphore_signal(
            barrier, inc=1, device_id=(c, lax.rem(h + d, NB)), device_id_type=MESH
        )

    def remote(src, dst, send, recv, device):
        return pltpu.make_async_remote_copy(
            src, dst, send, recv, device_id=device, device_id_type=MESH
        )

    def y_copy(kind, src, dst, peer):
        return remote(src, dst, refs["y_send"].at[kind], refs["y_recv"].at[kind], (c, peer))

    def y_start(kind, src, dest):
        for d in range(1, NB):
            to = lax.rem(h + d, NB)
            y_copy(kind, src.at[to], dest.at[h], to).start()
        dest[h] = src[h]

    def y_all(kind, src, dest):
        others = pl.ds(0, NB - 1)
        return y_copy(kind, src.at[others], dest.at[others], lax.rem(h + 1, NB))

    def y_wait(kind, src, dest):
        y_all(kind, src, dest).wait_recv()

    def project(rows, weight, dims, put):
        for p in range(4):
            if dims is NN:
                w = weight[:, p * 256 : (p + 1) * 256]
            else:
                w = weight[p * 256 : (p + 1) * 256, :]
            out = dot(rows[...], w, dims)
            put(2 * p, out[:, :BLK].T.astype(BF))
            put(2 * p + 1, out[:, BLK:].T.astype(BF))

    def put_heads(part):
        def put(dest, tile):
            refs["y_out"][part][0][dest] = tile[:HD]
            refs["y_out"][part][1][dest] = tile[HD:]

        return put

    def put_whole(n):
        def put(dest, tile):
            refs["qg_out"][n][dest] = tile

        return put

    def index_tables():
        kept = refs["kept"][...]
        fetched = jnp.maximum(kept - NB, 0)
        source = (fetched * 43) >> 7
        e = ((source >> 2) - x + SIDE) & 3
        f = ((source & 3) - z + SIDE) & 3
        relative = NB + (e * SIDE + f) * SLOT + fetched - source * SLOT
        slots = jnp.where(kept < NB, kept, relative)
        row = lax.broadcasted_iota(jnp.int32, (NB, NB), 0)
        limit = jnp.zeros((NB, NB), jnp.int32)
        for b in range(NB):
            limit = jnp.where(row == b, count[b], limit)
        column = lax.broadcasted_iota(jnp.int32, (NB, NB), 1)
        slots = jnp.where(column < limit, slots, row)
        lane = lax.broadcasted_iota(jnp.int32, (NB, BLK), 1)
        wide_row = lax.broadcasted_iota(jnp.int32, (NB, BLK), 0)
        entry_of = jnp.full((NB, BLK), LIVE, jnp.int32)
        for j in range(NB):
            hit = (slots[:, j : j + 1] == lane) & (limit[:, j : j + 1] > j)
            entry_of = jnp.where(hit, wide_row * NB + j, entry_of)
        refs["index_v"][0:NB] = jnp.zeros((NB, BLK), jnp.int32)
        refs["index_v"][0:NB, 0:NB] = slots
        refs["index_v"][NB : 2 * NB] = entry_of
        copy = load(6, refs["index_v"], index)
        copy.start()
        return copy

    index_copy = index_tables()
    load_feat.wait()
    load_k.wait()
    project(feat, refs["w"][0], NN, put_heads(0))
    pl.semaphore_wait(barrier, 6 + NB - 1)
    y_start(0, refs["y_out"][0][0], first[0][0][0])
    load_gout.start()
    load_q.start()
    load_o.start()
    load_v.wait()
    project(feat, refs["w"][1], NN, put_heads(1))
    y_start(2, refs["y_out"][1][0], first[1][0][0])
    y_start(1, refs["y_out"][0][1], first[0][1][0])
    y_start(3, refs["y_out"][1][1], first[1][1][0])
    load_q.wait()
    project(feat, refs["w"][2], NN, put_whole(0))
    y_start(4, refs["qg_out"][0], refs["qg"][0])
    load_gout.wait()
    load_o.wait()
    project(gout, refs["w"][3], NT, put_whole(1))
    y_start(5, refs["qg_out"][1], refs["qg"][1])
    index_copy.wait()

    def spread_copy(hh, part, src, e, blocks, to):
        return remote(
            first[part][hh][src].at[blocks], first[part][hh][e].at[blocks],
            refs["f_send"].at[hh, part], refs["f_recv"].at[hh, part, e - 1],
            (at(part, to, 0), h),
        )

    def spread_wait(hh, part, e):
        spread_copy(hh, part, 0, e, pl.ds(0, NB), e).wait_recv()

    def pick_copy(hh, part, d, e):
        return remote(
            stage[part][hh].at[d - 1, e],
            table[part][hh].at[pl.ds(base(part, d, e), SLOT)],
            refs["s_send"].at[hh, part], refs["s_recv"].at[hh, part],
            (at(part, 0, back_by(d)), h),
        )

    def pick(hh, part, e):
        source = at(part, e, 0)
        for d in NEAR:
            reader = at(part, 0, back_by(d))
            for r in range(SLOT):
                stage[part][hh][d - 1, e, r] = first[part][hh][e][fetch[r, reader, source]]
            pick_copy(hh, part, d, e).start()

    def keep(hh, part, e):
        if e == 0:
            for t in range(NB):
                table[part][hh][t] = first[part][hh][0][t]
        else:
            source = at(part, e, 0)
            for r in range(SLOT):
                table[part][hh][base(part, 0, e) + r] = first[part][hh][e][fetch[r, c, source]]

    def forward_start(hh):
        for part in range(2):
            y_wait(2 * part + hh, refs["y_out"][part][hh], first[part][hh][0])
            for e in (1, 3):
                spread_copy(hh, part, 0, e, pl.ds(0, NB), back_by(e)).start()
            pick(hh, part, 0)
        for part in range(2):
            keep(hh, part, 0)

    def forward_step(hh, e):
        for part in range(2):
            spread_wait(hh, part, e)
            if e == 1:
                spread_copy(hh, part, 1, 2, pl.ds(0, NB // 2), 3).start()
            if e == 3:
                spread_copy(hh, part, 3, 2, pl.ds(NB // 2, NB // 2), 1).start()
            pick(hh, part, e)
            keep(hh, part, e)

    def stand_in(part, hh, send, recv, blocks):
        some = table[part][hh].at[pl.ds(0, blocks)]
        return remote(some, some, send.at[hh, part], recv.at[hh, part], (at(part, 1, 0), h))

    def forward_done(hh):
        for part in range(2):
            stand_in(part, hh, refs["s_send"], refs["s_recv"], 3 * SIDE * SLOT).wait_recv()

    def attention(hh, hooks):
        half = slice(hh * HD, (hh + 1) * HD)

        def block(b, _):
            for when, hook in hooks.items():
                pl.when(b == when)(hook)
            n = count[b]
            slots = [index[b, j] for j in range(NB)]
            kc = jnp.concatenate([table[0][hh][i] for i in slots], axis=1)
            vc = jnp.concatenate([table[1][hh][i] for i in slots], axis=1)
            q_t = refs["qg"][0][b, half, :].astype(F32) * 0.125
            g_t = refs["qg"][1][b, half, :].astype(F32)
            q = q_t.T.astype(BF)
            g32 = g_t.T
            g = g32.astype(BF)
            s = dot(q, kc)
            s = jnp.concatenate(
                [jnp.where(j < n, s[:, j * BLK : (j + 1) * BLK], -jnp.inf) for j in range(NB)],
                axis=1,
            )
            p = jnp.exp(s - jnp.max(s, axis=1, keepdims=True))
            a = p * (1.0 / jnp.sum(p, axis=1, keepdims=True))
            low = a.astype(BF)
            attn = dot(low, vc, NT).astype(BF)
            delta = jnp.sum(g32 * attn.astype(F32), axis=1, keepdims=True)
            ds = (a * (dot(g, vc) - delta)).astype(BF)
            dq = (dot(ds, kc, NT) * 0.125).astype(BF)
            dk_t = dot(q_t.astype(BF), ds)
            dv_t = dot(g_t.astype(BF), low)
            for j in range(NB):
                cols = slice(j * BLK, (j + 1) * BLK)
                terms[0][b * NB + j] = dk_t[:, cols]
                terms[1][b * NB + j] = dv_t[:, cols]
            if hh == 0:
                refs["half"][0][b] = attn
                refs["half"][1][b] = dq
            else:
                refs["row_out"][0][b] = jnp.concatenate([refs["half"][0][b], attn], axis=1)
                refs["row_out"][1][b] = jnp.concatenate([refs["half"][1][b], dq], axis=1)
            return 0

        lax.fori_loop(0, NB, block, 0)

    def slot_total(part, slot):
        acc = terms[part][index[NB, slot]]
        for b in range(1, NB):
            acc = acc + terms[part][index[NB + b, slot]]
        return acc

    def slot_copy(hh, part, d, e):
        return remote(
            slot_out[part][hh].at[d - 1, e],
            got[part][hh][e].at[pl.ds((d - 1) * SLOT, SLOT)],
            refs["g_send"].at[hh, part], refs["g_recv"].at[hh, part, e],
            (at(part, 0, d), h),
        )

    def backward_start(hh):
        for e in OUTWARD:
            for d in NEAR:
                for part in range(2):

                    def one(r, _, e=e, d=d, part=part):
                        total = slot_total(part, base(part, d, e) + r)
                        slot_out[part][hh][d - 1, e, r] = total.astype(BF)
                        return 0

                    lax.fori_loop(0, SLOT, one, 0)
                    slot_copy(hh, part, d, e).start()
        for part in range(2):
            for e in (1, 2, 3):

                def near(r, _, e=e, part=part):
                    total = slot_total(part, base(part, 0, e) + r)
                    got[part][hh][e][9 + r] = total.astype(BF)
                    return 0

                lax.fori_loop(0, SLOT, near, 0)

            def own(t, _, part=part):
                own_sum[part][hh][t] = slot_total(part, t)
                return 0

            lax.fori_loop(0, NB, own, 0)

    def back_copy(hh, part, e):
        return remote(
            back_out[part][hh].at[e - 1], back_in[part][hh].at[e - 1],
            refs["b_send"].at[hh, part], refs["b_recv"].at[hh, part],
            (at(part, e, 0), h),
        )

    def backward_step(hh, e):
        for part in range(2):
            some = got[part][hh][e].at[pl.ds(0, 3 * SLOT)]
            remote(
                some, some, refs["g_send"].at[hh, part], refs["g_recv"].at[hh, part, e],
                (at(part, 0, 1), h),
            ).wait_recv()
            source = at(part, e, 0)

            def one(t, _, part=part, source=source):
                acc = own_sum[part][hh][t] if e == 0 else None
                for d in (0, 1, 2, 3):
                    if d == 0 and e == 0:
                        continue
                    reader = at(part, 0, back_by(d))
                    place = 12
                    for r in range(SLOT):
                        here = (9 if d == 0 else (d - 1) * SLOT) + r
                        place = jnp.where(fetch[r, reader, source] == t, here, place)
                    term = got[part][hh][e][place].astype(F32)
                    acc = term if acc is None else acc + term
                if e == 0:
                    own_sum[part][hh][t] = acc
                else:
                    back_out[part][hh][e - 1, t] = acc.astype(BF)
                return 0

            lax.fori_loop(0, NB, one, 0)
            if e:
                back_copy(hh, part, e).start()

    def backward_finish(hh):
        for part in range(2):
            stand_in(part, hh, refs["b_send"], refs["b_recv"], 3 * NB).wait_recv()

            def one(t, _, part=part):
                acc = own_sum[part][hh][t]
                for e in range(3):
                    acc = acc + back_in[part][hh][e, t].astype(F32)
                final[part][hh][t] = acc.astype(BF)
                return 0

            lax.fori_loop(0, NB, one, 0)
            y_start(8 + 2 * part + hh, final[part][hh], refs["grads"][part][hh])

    forward_start(0)
    for e in NEAR:
        forward_step(0, e)
    forward_start(1)
    for part in range(2):
        terms[part][LIVE] = jnp.zeros((HD, BLK), F32)
        for hh in range(2):
            for e in range(SIDE):
                got[part][hh][e][12] = jnp.zeros((HD, BLK), BF)
    y_wait(4, refs["qg_out"][0], refs["qg"][0])
    y_wait(5, refs["qg_out"][1], refs["qg"][1])
    forward_done(0)
    attention(0, {n + 1: (lambda e=e: forward_step(1, e)) for n, e in enumerate(NEAR)})
    backward_start(0)
    forward_done(1)
    attention(1, {n + 2: (lambda e=e: backward_step(0, e)) for n, e in enumerate(OUTWARD)})
    backward_start(1)
    y_start(6, refs["row_out"][0], refs["rows"][0])
    y_start(7, refs["row_out"][1], refs["rows"][1])
    backward_finish(0)

    def wide(ref):
        return jnp.concatenate([ref[i] for i in range(NB)], axis=1)

    def wide_t(part):
        tiles = []
        for i in range(NB):
            tile = jnp.concatenate([refs["grads"][part][hh][i] for hh in range(2)], axis=0)
            tiles.append(tile.astype(F32).T.astype(BF))
        return jnp.concatenate(tiles, axis=1)

    y_wait(6, refs["row_out"][0], refs["rows"][0])
    refs["att"][...] = dot(wide(refs["rows"][0]), refs["w"][3][...]).astype(BF)
    save_att = load(0, refs["att"], refs["attended"])
    save_att.start()
    y_wait(7, refs["row_out"][1], refs["rows"][1])
    refs["grad"][...] = dot(wide(refs["rows"][1]), refs["w"][2][...], NT)
    for e in OUTWARD:
        backward_step(1, e)
    backward_finish(1)
    for part in range(2):
        for hh in range(2):
            y_wait(8 + 2 * part + hh, final[part][hh], refs["grads"][part][hh])
        term = dot(wide_t(part), refs["w"][part][...], NT)
        if part == 0:
            refs["grad"][...] += term
        else:
            refs["gf"][...] = (refs["grad"][...] + term).astype(BF)
    save_gf = load(1, refs["gf"], refs["grad_features"])
    save_gf.start()
    for part in range(2):
        y_all(4 + part, refs["qg_out"][part], refs["qg"][part]).wait_send()
        y_all(6 + part, refs["row_out"][part], refs["rows"][part]).wait_send()
        for hh in range(2):
            y_all(2 * part + hh, refs["y_out"][part][hh], first[part][hh][0]).wait_send()
            y_all(8 + 2 * part + hh, final[part][hh], refs["grads"][part][hh]).wait_send()
            for name, blocks in (("f", 24), ("s", 36), ("g", 36), ("b", 24)):
                stand_in(part, hh, refs[name + "_send"], refs["s_recv"], blocks).wait_send()
    save_att.wait()
    save_gf.wait()


def copy_kernel(attended, grad_features, attended_out, grad_features_out):
    attended_out[...] = attended[...]
    grad_features_out[...] = grad_features[...]


def tree_call(layout, kernel):
    flat, tree = jax.tree.flatten(layout, is_leaf=lambda leaf: not isinstance(leaf, (list, dict)))

    def called(names, *refs):
        kernel({**names, **jax.tree.unflatten(tree, refs)})

    return flat, called


def shards(features, grad_out, w_qkv, w_out, kept_slot, kept_count, fetch_slots):
    dma = pltpu.SemaphoreType.DMA
    def vm(*shape, dtype=BF):
        return pltpu.VMEM(shape, dtype)

    def each(make, *counts):
        if not counts:
            return make()
        return [each(make, *counts[1:]) for _ in range(counts[0])]

    tile = (HD, BLK)
    layout = {
        "w": each(lambda: vm(1024, 1024), 4),
        "y_out": each(lambda: vm(NB, *tile), 2, 2),
        "qg_out": each(lambda: vm(NB, BLK, BLK), 2),
        "qg": each(lambda: vm(NB, BLK, BLK), 2),
        "first": each(lambda: vm(NB, *tile), 2, 2, SIDE),
        "table": each(lambda: vm(TABLE, *tile), 2, 2),
        "stage": each(lambda: vm(3, SIDE, SLOT, *tile), 2, 2),
        "terms": each(lambda: vm(LIVE + 1, *tile, dtype=F32), 2),
        "half": each(lambda: vm(NB, BLK, HD), 2),
        "row_out": each(lambda: vm(NB, BLK, BLK), 2),
        "rows": each(lambda: vm(NB, BLK, BLK), 2),
        "slot_out": each(lambda: vm(3, SIDE, SLOT, *tile), 2, 2),
        "got": each(lambda: vm(13, *tile), 2, 2, SIDE),
        "own_sum": each(lambda: vm(NB, *tile, dtype=F32), 2, 2),
        "back_out": each(lambda: vm(3, NB, *tile), 2, 2),
        "back_in": each(lambda: vm(3, NB, *tile), 2, 2),
        "final": each(lambda: vm(NB, *tile), 2, 2),
        "grads": each(lambda: vm(NB, *tile), 2, 2),
        "grad": vm(BLK, 1024, dtype=F32),
        "feat": vm(BLK, 1024),
        "gout": vm(BLK, 1024),
        "att": vm(BLK, 1024),
        "gf": vm(BLK, 1024),
        "index_v": vm(2 * NB, BLK, dtype=jnp.int32),
        "index": pltpu.SMEM((2 * NB, BLK), jnp.int32),
        "w_sem": dma((7,)),
        "y_send": dma((12,)),
        "y_recv": dma((12,)),
        "f_send": dma((2, 2)),
        "f_recv": dma((2, 2, 3)),
        "s_send": dma((2, 2)),
        "s_recv": dma((2, 2)),
        "g_send": dma((2, 2)),
        "g_recv": dma((2, 2, SIDE)),
        "b_send": dma((2, 2)),
        "b_recv": dma((2, 2)),
    }
    scratch, called = tree_call(layout, sublayer_kernel)
    names = ("feat_in", "gout_in", "wqkv", "wout", "kept", "count", "fetch")
    names += ("attended", "grad_features")

    def kernel(*refs):
        called(dict(zip(names, refs)), *refs[len(names) :])

    near = pl.BlockSpec(memory_space=pltpu.VMEM)
    far = pl.BlockSpec(memory_space=pl.ANY)
    scalars = pl.BlockSpec(memory_space=pltpu.SMEM)
    out_shape = [jax.ShapeDtypeStruct(features.shape, BF)] * 2
    results = pl.pallas_call(
        kernel,
        out_shape=out_shape,
        in_specs=[far, far, far, far, near, scalars, scalars],
        out_specs=[far, far],
        scratch_shapes=scratch,
        compiler_params=pltpu.CompilerParams(
            collective_id=0, has_side_effects=True, vmem_limit_bytes=VMEM_LIMIT
        ),
    )(
        features, grad_out, w_qkv, w_out, kept_slot, kept_count,
        jnp.transpose(fetch_slots, (2, 0, 1)),
    )
    return pl.pallas_call(
        copy_kernel, out_shape=out_shape, in_specs=[near, near], out_specs=[near, near]
    )(*results)


def solution(mesh):
    rows = P(("cluster", "head"), None)
    in_specs = (rows, rows, P(), P(), P("cluster", None), P("cluster"), P())
    return jax.shard_map(
        shards, mesh=mesh, in_specs=in_specs, out_specs=(rows, rows), check_vma=False
    )
```

```python
import jax
import jax.numpy as jnp
from jax import lax
from jax.experimental import pallas as pl
from jax.experimental.pallas import tpu as pltpu
from jax.sharding import PartitionSpec as P

MESH = pl.DeviceIdType.MESH
BF = jnp.bfloat16
F32 = jnp.float32
BLK = 128
HD = 64
NB = 8
SIDE = 4
SLOT = 3
TABLE = NB + SIDE * SIDE * SLOT
GROUP = 4
LIVE = NB * NB
NEAR = (1, 3, 2)
OUTWARD = (2, 1, 3, 0)
VMEM_LIMIT = 56 << 20

NN = (((1,), (0,)), ((), ()))
NT = (((1,), (1,)), ((), ()))


def dot(a, b, dims=NN):
    return lax.dot_general(a, b, dims, preferred_element_type=F32)


def back_by(d):
    return (SIDE - d) % SIDE


def base(part, d, e):
    return NB + ((e * SIDE + d) if part == 0 else (d * SIDE + e)) * SLOT


def sublayer_kernel(refs):
    feat, gout, wqkv, wout = refs["feat"], refs["gout"], refs["wqkv"], refs["wout"]
    index, count, fetch = refs["index"], refs["count"], refs["fetch"]
    first, table, stage = refs["first"], refs["table"], refs["stage"]
    terms, slot_out, got = refs["terms"], refs["slot_out"], refs["got"]
    own_sum, back_out, back_in = refs["own_sum"], refs["back_out"], refs["back_in"]
    final = refs["final"]
    c = lax.axis_index("cluster")
    h = lax.axis_index("head")
    x, z = c // SIDE, c % SIDE

    def at(part, a, b):
        if part == 1:
            a, b = b, a
        return lax.rem(x + a, SIDE) * SIDE + lax.rem(z + b, SIDE)

    def load(n, src, dst):
        return pltpu.make_async_copy(src, dst, refs["w_sem"].at[n])

    loads = [load(4, refs["feat_in"], feat), load(5, refs["gout_in"], gout)]
    for n, piece in enumerate((1, 2, 0)):
        loads.append(load(n, wqkv.at[:, pl.ds(piece * 1024, 1024)], refs["w"][n]))
    loads.append(load(3, wout, refs["w"][3]))
    load_feat, load_gout, load_k, load_v, load_q, load_o = loads
    load_feat.start()
    load_k.start()
    load_v.start()

    barrier = pltpu.get_barrier_semaphore()
    for d in (1, 2, 3):
        for part in range(2):
            pl.semaphore_signal(
                barrier, inc=1, device_id=(at(part, d, 0), h), device_id_type=MESH
            )
    for d in range(1, NB):
        pl.semaphore_signal(
            barrier, inc=1, device_id=(c, lax.rem(h + d, NB)), device_id_type=MESH
        )

    def remote(src, dst, send, recv, device):
        return pltpu.make_async_remote_copy(
            src, dst, send, recv, device_id=device, device_id_type=MESH
        )

    def y_copy(kind, src, dst, peer):
        return remote(src, dst, refs["y_send"].at[kind], refs["y_recv"].at[kind], (c, peer))

    def y_start(kind, src, dest):
        for d in range(1, NB):
            to = lax.rem(h + d, NB)
            y_copy(kind, src.at[to], dest.at[h], to).start()
        dest[h] = src[h]

    def y_all(kind, src, dest):
        others = pl.ds(0, NB - 1)
        return y_copy(kind, src.at[others], dest.at[others], lax.rem(h + 1, NB))

    def y_wait(kind, src, dest):
        y_all(kind, src, dest).wait_recv()

    def project(rows, weight, dims, put):
        for p in range(4):
            if dims is NN:
                w = weight[:, p * 256 : (p + 1) * 256]
            else:
                w = weight[p * 256 : (p + 1) * 256, :]
            out = dot(rows[...], w, dims)
            put(2 * p, out[:, :BLK].T.astype(BF))
            put(2 * p + 1, out[:, BLK:].T.astype(BF))

    def put_heads(part):
        def put(dest, tile):
            refs["y_out"][part][0][dest] = tile[:HD]
            refs["y_out"][part][1][dest] = tile[HD:]

        return put

    def put_whole(n):
        def put(dest, tile):
            refs["qg_out"][n][dest] = tile

        return put

    def index_tables():
        kept = refs["kept"][...]
        fetched = jnp.maximum(kept - NB, 0)
        source = (fetched * 43) >> 7
        e = ((source >> 2) - x + SIDE) & 3
        f = ((source & 3) - z + SIDE) & 3
        relative = NB + (e * SIDE + f) * SLOT + fetched - source * SLOT
        slots = jnp.where(kept < NB, kept, relative)
        row = lax.broadcasted_iota(jnp.int32, (NB, NB), 0)
        limit = jnp.zeros((NB, NB), jnp.int32)
        for b in range(NB):
            limit = jnp.where(row == b, count[b], limit)
        column = lax.broadcasted_iota(jnp.int32, (NB, NB), 1)
        slots = jnp.where(column < limit, slots, row)
        lane = lax.broadcasted_iota(jnp.int32, (NB, BLK), 1)
        wide_row = lax.broadcasted_iota(jnp.int32, (NB, BLK), 0)
        entry_of = jnp.full((NB, BLK), LIVE, jnp.int32)
        for j in range(NB):
            hit = (slots[:, j : j + 1] == lane) & (limit[:, j : j + 1] > j)
            entry_of = jnp.where(hit, wide_row * NB + j, entry_of)
        refs["index_v"][0:NB] = jnp.zeros((NB, BLK), jnp.int32)
        refs["index_v"][0:NB, 0:NB] = slots
        refs["index_v"][NB : 2 * NB] = entry_of
        copy = load(6, refs["index_v"], index)
        copy.start()
        return copy

    index_copy = index_tables()
    load_feat.wait()
    load_k.wait()
    project(feat, refs["w"][0], NN, put_heads(0))
    pl.semaphore_wait(barrier, 6 + NB - 1)
    y_start(0, refs["y_out"][0][0], first[0][0][0])
    load_gout.start()
    load_q.start()
    load_o.start()
    load_v.wait()
    project(feat, refs["w"][1], NN, put_heads(1))
    y_start(2, refs["y_out"][1][0], first[1][0][0])
    y_start(1, refs["y_out"][0][1], first[0][1][0])
    y_start(3, refs["y_out"][1][1], first[1][1][0])
    load_q.wait()
    project(feat, refs["w"][2], NN, put_whole(0))
    y_start(4, refs["qg_out"][0], refs["qg"][0])
    load_gout.wait()
    load_o.wait()
    project(gout, refs["w"][3], NT, put_whole(1))
    y_start(5, refs["qg_out"][1], refs["qg"][1])
    index_copy.wait()

    def spread_copy(hh, part, src, e, blocks, to):
        return remote(
            first[part][hh][src].at[blocks], first[part][hh][e].at[blocks],
            refs["f_send"].at[hh, part], refs["f_recv"].at[hh, part, e - 1],
            (at(part, to, 0), h),
        )

    def spread_wait(hh, part, e):
        spread_copy(hh, part, 0, e, pl.ds(0, NB), e).wait_recv()

    def pick_copy(hh, part, d, e):
        return remote(
            stage[part][hh].at[d - 1, e],
            table[part][hh].at[pl.ds(base(part, d, e), SLOT)],
            refs["s_send"].at[hh, part], refs["s_recv"].at[hh, part],
            (at(part, 0, back_by(d)), h),
        )

    def pick(hh, part, e):
        source = at(part, e, 0)
        for d in NEAR:
            reader = at(part, 0, back_by(d))
            for r in range(SLOT):
                stage[part][hh][d - 1, e, r] = first[part][hh][e][fetch[r, reader, source]]
            pick_copy(hh, part, d, e).start()

    def keep(hh, part, e):
        if e == 0:
            for t in range(NB):
                table[part][hh][t] = first[part][hh][0][t]
        else:
            source = at(part, e, 0)
            for r in range(SLOT):
                table[part][hh][base(part, 0, e) + r] = first[part][hh][e][fetch[r, c, source]]

    def forward_start(hh):
        for part in range(2):
            y_wait(2 * part + hh, refs["y_out"][part][hh], first[part][hh][0])
            for e in (1, 3):
                spread_copy(hh, part, 0, e, pl.ds(0, NB), back_by(e)).start()
            pick(hh, part, 0)
        for part in range(2):
            keep(hh, part, 0)

    def forward_step(hh, e):
        for part in range(2):
            spread_wait(hh, part, e)
            if e == 1:
                spread_copy(hh, part, 1, 2, pl.ds(0, NB // 2), 3).start()
            if e == 3:
                spread_copy(hh, part, 3, 2, pl.ds(NB // 2, NB // 2), 1).start()
            pick(hh, part, e)
            keep(hh, part, e)

    def stand_in(part, hh, send, recv, blocks):
        some = table[part][hh].at[pl.ds(0, blocks)]
        return remote(some, some, send.at[hh, part], recv.at[hh, part], (at(part, 1, 0), h))

    def forward_done(hh):
        for part in range(2):
            stand_in(part, hh, refs["s_send"], refs["s_recv"], 3 * SIDE * SLOT).wait_recv()

    def attention(hh):
        half = slice(hh * HD, (hh + 1) * HD)

        def load_block(b):
            slots = [index[b, j] for j in range(NB)]
            kc = jnp.concatenate([table[0][hh][i] for i in slots], axis=1)
            vc = jnp.concatenate([table[1][hh][i] for i in slots], axis=1)
            q_t = refs["qg"][0][b, half, :].astype(F32) * 0.125
            g_t = refs["qg"][1][b, half, :].astype(F32)
            return kc, vc, q_t, g_t

        def block(i, _):
            blocks = [i * GROUP + n for n in range(GROUP)]
            loaded = [load_block(b) for b in blocks]
            scores = []
            for b, (kc, vc, q_t, g_t) in zip(blocks, loaded):
                s = dot(q_t.T.astype(BF), kc)
                n = count[b]
                scores.append(
                    jnp.concatenate(
                        [
                            jnp.where(j < n, s[:, j * BLK : (j + 1) * BLK], -jnp.inf)
                            for j in range(NB)
                        ],
                        axis=1,
                    )
                )
            probs = []
            for s in scores:
                p = jnp.exp(s - jnp.max(s, axis=1, keepdims=True))
                probs.append(p * (1.0 / jnp.sum(p, axis=1, keepdims=True)))
            lows = [a.astype(BF) for a in probs]
            attns = [dot(low, vc, NT).astype(BF) for low, (_, vc, _, _) in zip(lows, loaded)]
            grads = []
            for a, attn, (kc, vc, q_t, g_t) in zip(probs, attns, loaded):
                g = g_t.T
                delta = jnp.sum(g * attn.astype(F32), axis=1, keepdims=True)
                grads.append((a * (dot(g.astype(BF), vc) - delta)).astype(BF))
            for b, low, ds, attn, (kc, vc, q_t, g_t) in zip(blocks, lows, grads, attns, loaded):
                dq = (dot(ds, kc, NT) * 0.125).astype(BF)
                dk_t = dot(q_t.astype(BF), ds)
                dv_t = dot(g_t.astype(BF), low)
                for j in range(NB):
                    cols = slice(j * BLK, (j + 1) * BLK)
                    terms[0][b * NB + j] = dk_t[:, cols]
                    terms[1][b * NB + j] = dv_t[:, cols]
                if hh == 0:
                    refs["half"][0][b] = attn
                    refs["half"][1][b] = dq
                else:
                    refs["row_out"][0][b] = jnp.concatenate([refs["half"][0][b], attn], axis=1)
                    refs["row_out"][1][b] = jnp.concatenate([refs["half"][1][b], dq], axis=1)
            return 0

        lax.fori_loop(0, NB // GROUP, block, 0)

    def slot_total(part, slot):
        acc = terms[part][index[NB, slot]]
        for b in range(1, NB):
            acc = acc + terms[part][index[NB + b, slot]]
        return acc

    def slot_copy(hh, part, d, e):
        return remote(
            slot_out[part][hh].at[d - 1, e],
            got[part][hh][e].at[pl.ds((d - 1) * SLOT, SLOT)],
            refs["g_send"].at[hh, part], refs["g_recv"].at[hh, part, e],
            (at(part, 0, d), h),
        )

    def backward_start(hh):
        for e in OUTWARD:
            for d in NEAR:
                for part in range(2):

                    def one(r, _, e=e, d=d, part=part):
                        total = slot_total(part, base(part, d, e) + r)
                        slot_out[part][hh][d - 1, e, r] = total.astype(BF)
                        return 0

                    lax.fori_loop(0, SLOT, one, 0)
                    slot_copy(hh, part, d, e).start()
        for part in range(2):
            for e in (1, 2, 3):

                def near(r, _, e=e, part=part):
                    total = slot_total(part, base(part, 0, e) + r)
                    got[part][hh][e][9 + r] = total.astype(BF)
                    return 0

                lax.fori_loop(0, SLOT, near, 0)

            def own(t, _, part=part):
                own_sum[part][hh][t] = slot_total(part, t)
                return 0

            lax.fori_loop(0, NB, own, 0)

    def back_copy(hh, part, e):
        return remote(
            back_out[part][hh].at[e - 1], back_in[part][hh].at[e - 1],
            refs["b_send"].at[hh, part], refs["b_recv"].at[hh, part],
            (at(part, e, 0), h),
        )

    def backward_step(hh, e):
        for part in range(2):
            some = got[part][hh][e].at[pl.ds(0, 3 * SLOT)]
            remote(
                some, some, refs["g_send"].at[hh, part], refs["g_recv"].at[hh, part, e],
                (at(part, 0, 1), h),
            ).wait_recv()
            source = at(part, e, 0)

            def one(t, _, part=part, source=source):
                acc = own_sum[part][hh][t] if e == 0 else None
                for d in (0, 1, 2, 3):
                    if d == 0 and e == 0:
                        continue
                    reader = at(part, 0, back_by(d))
                    place = 12
                    for r in range(SLOT):
                        here = (9 if d == 0 else (d - 1) * SLOT) + r
                        place = jnp.where(fetch[r, reader, source] == t, here, place)
                    term = got[part][hh][e][place].astype(F32)
                    acc = term if acc is None else acc + term
                if e == 0:
                    own_sum[part][hh][t] = acc
                else:
                    back_out[part][hh][e - 1, t] = acc.astype(BF)
                return 0

            lax.fori_loop(0, NB, one, 0)
            if e:
                back_copy(hh, part, e).start()

    def backward_finish(hh):
        for part in range(2):
            stand_in(part, hh, refs["b_send"], refs["b_recv"], 3 * NB).wait_recv()

            def one(t, _, part=part):
                acc = own_sum[part][hh][t]
                for e in range(3):
                    acc = acc + back_in[part][hh][e, t].astype(F32)
                final[part][hh][t] = acc.astype(BF)
                return 0

            lax.fori_loop(0, NB, one, 0)
            y_start(8 + 2 * part + hh, final[part][hh], refs["grads"][part][hh])

    forward_start(0)
    for e in NEAR:
        forward_step(0, e)
    forward_start(1)
    for part in range(2):
        terms[part][LIVE] = jnp.zeros((HD, BLK), F32)
        for hh in range(2):
            for e in range(SIDE):
                got[part][hh][e][12] = jnp.zeros((HD, BLK), BF)
    y_wait(4, refs["qg_out"][0], refs["qg"][0])
    y_wait(5, refs["qg_out"][1], refs["qg"][1])
    forward_step(1, 1)
    forward_step(1, 3)
    forward_done(0)
    attention(0)
    forward_step(1, 2)
    backward_start(0)
    forward_done(1)
    attention(1)
    backward_start(1)
    y_start(6, refs["row_out"][0], refs["rows"][0])
    y_start(7, refs["row_out"][1], refs["rows"][1])
    for e in OUTWARD:
        backward_step(0, e)
    backward_finish(0)

    def wide(ref):
        return jnp.concatenate([ref[i] for i in range(NB)], axis=1)

    def wide_t(part):
        tiles = []
        for i in range(NB):
            tile = jnp.concatenate([refs["grads"][part][hh][i] for hh in range(2)], axis=0)
            tiles.append(tile.astype(F32).T.astype(BF))
        return jnp.concatenate(tiles, axis=1)

    y_wait(6, refs["row_out"][0], refs["rows"][0])
    refs["att"][...] = dot(wide(refs["rows"][0]), refs["w"][3][...]).astype(BF)
    save_att = load(0, refs["att"], refs["attended"])
    save_att.start()
    y_wait(7, refs["row_out"][1], refs["rows"][1])
    refs["grad"][...] = dot(wide(refs["rows"][1]), refs["w"][2][...], NT)
    for e in OUTWARD:
        backward_step(1, e)
    backward_finish(1)
    for part in range(2):
        for hh in range(2):
            y_wait(8 + 2 * part + hh, final[part][hh], refs["grads"][part][hh])
        term = dot(wide_t(part), refs["w"][part][...], NT)
        if part == 0:
            refs["grad"][...] += term
        else:
            refs["gf"][...] = (refs["grad"][...] + term).astype(BF)
    save_gf = load(1, refs["gf"], refs["grad_features"])
    save_gf.start()
    for part in range(2):
        y_all(4 + part, refs["qg_out"][part], refs["qg"][part]).wait_send()
        y_all(6 + part, refs["row_out"][part], refs["rows"][part]).wait_send()
        for hh in range(2):
            y_all(2 * part + hh, refs["y_out"][part][hh], first[part][hh][0]).wait_send()
            y_all(8 + 2 * part + hh, final[part][hh], refs["grads"][part][hh]).wait_send()
            for name, blocks in (("f", 24), ("s", 36), ("g", 36), ("b", 24)):
                stand_in(part, hh, refs[name + "_send"], refs["s_recv"], blocks).wait_send()
    save_att.wait()
    save_gf.wait()


def copy_kernel(attended, grad_features, attended_out, grad_features_out):
    attended_out[...] = attended[...]
    grad_features_out[...] = grad_features[...]


def tree_call(layout, kernel):
    flat, tree = jax.tree.flatten(layout, is_leaf=lambda leaf: not isinstance(leaf, (list, dict)))

    def called(names, *refs):
        kernel({**names, **jax.tree.unflatten(tree, refs)})

    return flat, called


def shards(features, grad_out, w_qkv, w_out, kept_slot, kept_count, fetch_slots):
    dma = pltpu.SemaphoreType.DMA
    def vm(*shape, dtype=BF):
        return pltpu.VMEM(shape, dtype)

    def each(make, *counts):
        if not counts:
            return make()
        return [each(make, *counts[1:]) for _ in range(counts[0])]

    tile = (HD, BLK)
    layout = {
        "w": each(lambda: vm(1024, 1024), 4),
        "y_out": each(lambda: vm(NB, *tile), 2, 2),
        "qg_out": each(lambda: vm(NB, BLK, BLK), 2),
        "qg": each(lambda: vm(NB, BLK, BLK), 2),
        "first": each(lambda: vm(NB, *tile), 2, 2, SIDE),
        "table": each(lambda: vm(TABLE, *tile), 2, 2),
        "stage": each(lambda: vm(3, SIDE, SLOT, *tile), 2, 2),
        "terms": each(lambda: vm(LIVE + 1, *tile, dtype=F32), 2),
        "half": each(lambda: vm(NB, BLK, HD), 2),
        "row_out": each(lambda: vm(NB, BLK, BLK), 2),
        "rows": each(lambda: vm(NB, BLK, BLK), 2),
        "slot_out": each(lambda: vm(3, SIDE, SLOT, *tile), 2, 2),
        "got": each(lambda: vm(13, *tile), 2, 2, SIDE),
        "own_sum": each(lambda: vm(NB, *tile, dtype=F32), 2, 2),
        "back_out": each(lambda: vm(3, NB, *tile), 2, 2),
        "back_in": each(lambda: vm(3, NB, *tile), 2, 2),
        "final": each(lambda: vm(NB, *tile), 2, 2),
        "grads": each(lambda: vm(NB, *tile), 2, 2),
        "grad": vm(BLK, 1024, dtype=F32),
        "feat": vm(BLK, 1024),
        "gout": vm(BLK, 1024),
        "att": vm(BLK, 1024),
        "gf": vm(BLK, 1024),
        "index_v": vm(2 * NB, BLK, dtype=jnp.int32),
        "index": pltpu.SMEM((2 * NB, BLK), jnp.int32),
        "w_sem": dma((7,)),
        "y_send": dma((12,)),
        "y_recv": dma((12,)),
        "f_send": dma((2, 2)),
        "f_recv": dma((2, 2, 3)),
        "s_send": dma((2, 2)),
        "s_recv": dma((2, 2)),
        "g_send": dma((2, 2)),
        "g_recv": dma((2, 2, SIDE)),
        "b_send": dma((2, 2)),
        "b_recv": dma((2, 2)),
    }
    scratch, called = tree_call(layout, sublayer_kernel)
    names = ("feat_in", "gout_in", "wqkv", "wout", "kept", "count", "fetch")
    names += ("attended", "grad_features")

    def kernel(*refs):
        called(dict(zip(names, refs)), *refs[len(names) :])

    near = pl.BlockSpec(memory_space=pltpu.VMEM)
    far = pl.BlockSpec(memory_space=pl.ANY)
    scalars = pl.BlockSpec(memory_space=pltpu.SMEM)
    out_shape = [jax.ShapeDtypeStruct(features.shape, BF)] * 2
    results = pl.pallas_call(
        kernel,
        out_shape=out_shape,
        in_specs=[far, far, far, far, near, scalars, scalars],
        out_specs=[far, far],
        scratch_shapes=scratch,
        compiler_params=pltpu.CompilerParams(
            collective_id=0, has_side_effects=True, vmem_limit_bytes=VMEM_LIMIT
        ),
    )(
        features, grad_out, w_qkv, w_out, kept_slot, kept_count,
        jnp.transpose(fetch_slots, (2, 0, 1)),
    )
    return pl.pallas_call(
        copy_kernel, out_shape=out_shape, in_specs=[near, near], out_specs=[near, near]
    )(*results)


def solution(mesh):
    rows = P(("cluster", "head"), None)
    in_specs = (rows, rows, P(), P(), P("cluster", None), P("cluster"), P())
    return jax.shard_map(
        shards, mesh=mesh, in_specs=in_specs, out_specs=(rows, rows), check_vma=False
    )
```

```python
import jax
import jax.numpy as jnp
from jax import lax
from jax.experimental import pallas as pl
from jax.experimental.pallas import tpu as pltpu
from jax.sharding import PartitionSpec as P

MESH = pl.DeviceIdType.MESH
BF = jnp.bfloat16
F32 = jnp.float32
BLK = 128
HD = 64
NB = 8
SIDE = 4
SLOT = 3
TABLE = NB + SIDE * SIDE * SLOT
GROUP = 4
LIVE = NB * NB
NEAR = (1, 3, 2)
OUTWARD = (2, 1, 3, 0)
VMEM_LIMIT = 56 << 20

NN = (((1,), (0,)), ((), ()))
NT = (((1,), (1,)), ((), ()))


def dot(a, b, dims=NN):
    return lax.dot_general(a, b, dims, preferred_element_type=F32)


def back_by(d):
    return (SIDE - d) % SIDE


def base(part, d, e):
    return NB + ((e * SIDE + d) if part == 0 else (d * SIDE + e)) * SLOT


def sublayer_kernel(refs):
    feat, gout, wqkv, wout = refs["feat"], refs["gout"], refs["wqkv"], refs["wout"]
    index, count, fetch = refs["index"], refs["count"], refs["fetch"]
    first, table, stage = refs["first"], refs["table"], refs["stage"]
    terms, slot_out, got = refs["terms"], refs["slot_out"], refs["got"]
    own_sum, back_out, back_in = refs["own_sum"], refs["back_out"], refs["back_in"]
    final = refs["final"]
    c = lax.axis_index("cluster")
    h = lax.axis_index("head")
    x, z = c // SIDE, c % SIDE

    def at(part, a, b):
        if part == 1:
            a, b = b, a
        return lax.rem(x + a, SIDE) * SIDE + lax.rem(z + b, SIDE)

    def load(n, src, dst):
        return pltpu.make_async_copy(src, dst, refs["w_sem"].at[n])

    loads = [load(4, refs["feat_in"], feat), load(5, refs["gout_in"], gout)]
    for n, piece in enumerate((1, 2, 0)):
        loads.append(load(n, wqkv.at[:, pl.ds(piece * 1024, 1024)], refs["w"][n]))
    loads.append(load(3, wout, refs["w"][3]))
    load_feat, load_gout, load_k, load_v, load_q, load_o = loads
    load_feat.start()
    load_k.start()
    load_v.start()

    barrier = pltpu.get_barrier_semaphore()
    for d in (1, 2, 3):
        for part in range(2):
            pl.semaphore_signal(
                barrier, inc=1, device_id=(at(part, d, 0), h), device_id_type=MESH
            )
    for d in range(1, NB):
        pl.semaphore_signal(
            barrier, inc=1, device_id=(c, lax.rem(h + d, NB)), device_id_type=MESH
        )

    def remote(src, dst, send, recv, device):
        return pltpu.make_async_remote_copy(
            src, dst, send, recv, device_id=device, device_id_type=MESH
        )

    def y_copy(kind, src, dst, peer):
        return remote(src, dst, refs["y_send"].at[kind], refs["y_recv"].at[kind], (c, peer))

    def y_start(kind, src, dest):
        for d in range(1, NB):
            to = lax.rem(h + d, NB)
            y_copy(kind, src.at[to], dest.at[h], to).start()
        dest[h] = src[h]

    def y_all(kind, src, dest):
        others = pl.ds(0, NB - 1)
        return y_copy(kind, src.at[others], dest.at[others], lax.rem(h + 1, NB))

    def y_wait(kind, src, dest):
        y_all(kind, src, dest).wait_recv()

    def project(rows, weight, dims, put):
        for p in range(4):
            if dims is NN:
                w = weight[:, p * 256 : (p + 1) * 256]
            else:
                w = weight[p * 256 : (p + 1) * 256, :]
            out = dot(rows[...], w, dims)
            put(2 * p, out[:, :BLK].T.astype(BF))
            put(2 * p + 1, out[:, BLK:].T.astype(BF))

    def put_heads(part):
        def put(dest, tile):
            refs["y_out"][part][0][dest] = tile[:HD]
            refs["y_out"][part][1][dest] = tile[HD:]

        return put

    def put_whole(n):
        def put(dest, tile):
            refs["qg_out"][n][dest] = tile

        return put

    def index_tables():
        kept = refs["kept"][...]
        fetched = jnp.maximum(kept - NB, 0)
        source = (fetched * 43) >> 7
        e = ((source >> 2) - x + SIDE) & 3
        f = ((source & 3) - z + SIDE) & 3
        relative = NB + (e * SIDE + f) * SLOT + fetched - source * SLOT
        slots = jnp.where(kept < NB, kept, relative)
        row = lax.broadcasted_iota(jnp.int32, (NB, NB), 0)
        limit = jnp.zeros((NB, NB), jnp.int32)
        for b in range(NB):
            limit = jnp.where(row == b, count[b], limit)
        column = lax.broadcasted_iota(jnp.int32, (NB, NB), 1)
        slots = jnp.where(column < limit, slots, row)
        lane = lax.broadcasted_iota(jnp.int32, (NB, BLK), 1)
        wide_row = lax.broadcasted_iota(jnp.int32, (NB, BLK), 0)
        entry_of = jnp.full((NB, BLK), LIVE, jnp.int32)
        for j in range(NB):
            hit = (slots[:, j : j + 1] == lane) & (limit[:, j : j + 1] > j)
            entry_of = jnp.where(hit, wide_row * NB + j, entry_of)
        refs["index_v"][0:NB] = jnp.zeros((NB, BLK), jnp.int32)
        refs["index_v"][0:NB, 0:NB] = slots
        refs["index_v"][NB : 2 * NB] = entry_of
        copy = load(6, refs["index_v"], index)
        copy.start()
        return copy

    def spread_copy(hh, part, src, e, blocks, to):
        if hh == 0:
            source = refs["spread"][part][src - 1] if src else refs["y_out"][part][0]
            target = refs["spread"][part][e - 1]
        else:
            source, target = first[part][1][src], first[part][1][e]
        return remote(
            source.at[blocks], target.at[blocks],
            refs["f_send"].at[hh, part], refs["f_recv"].at[hh, part, e - 1],
            (at(part, to, 0), h),
        )

    def spread_start(hh, part):
        for e in (1, 3):
            spread_copy(hh, part, 0, e, pl.ds(0, NB), back_by(e)).start()

    def spread_done(hh, part, e):
        spread_copy(hh, part, 0, e, pl.ds(0, NB), e).wait_recv()
        if e == 1:
            spread_copy(hh, part, 1, 2, pl.ds(0, NB // 2), 3).start()
        if e == 3:
            spread_copy(hh, part, 3, 2, pl.ds(NB // 2, NB // 2), 1).start()

    index_copy = index_tables()
    load_feat.wait()
    load_k.wait()
    project(feat, refs["w"][0], NN, put_heads(0))
    pl.semaphore_wait(barrier, 6 + NB - 1)
    spread_start(0, 0)
    y_start(0, refs["y_out"][0][0], first[0][0][0])
    load_gout.start()
    load_q.start()
    load_o.start()
    load_v.wait()
    project(feat, refs["w"][1], NN, put_heads(1))
    spread_start(0, 1)
    y_start(2, refs["y_out"][1][0], first[1][0][0])
    y_start(1, refs["y_out"][0][1], first[0][1][0])
    y_start(3, refs["y_out"][1][1], first[1][1][0])
    def pick_copy(hh, part, d, e):
        return remote(
            stage[part][hh].at[d - 1, e],
            table[part][hh].at[pl.ds(base(part, d, e), SLOT)],
            refs["s_send"].at[hh, part], refs["s_recv"].at[hh, part],
            (at(part, 0, back_by(d)), h),
        )

    def pick(hh, part, e):
        source = at(part, e, 0)
        for d in NEAR:
            reader = at(part, 0, back_by(d))
            for r in range(SLOT):
                stage[part][hh][d - 1, e, r] = first[part][hh][e][fetch[r, reader, source]]
            pick_copy(hh, part, d, e).start()

    def keep(hh, part, e):
        if e == 0:
            for t in range(NB):
                table[part][hh][t] = first[part][hh][0][t]
        else:
            source = at(part, e, 0)
            for r in range(SLOT):
                table[part][hh][base(part, 0, e) + r] = first[part][hh][e][fetch[r, c, source]]

    def far_kind(part, e):
        return 12 + 3 * part + e - 1

    def forward_first(e):
        for part in range(2):
            spread_done(0, part, e)
            y_start(far_kind(part, e), refs["spread"][part][e - 1], first[part][0][e])

    def forward_second(e):
        for part in range(2):
            kind = far_kind(part, e) if e else 2 * part
            source = refs["spread"][part][e - 1] if e else refs["y_out"][part][0]
            y_wait(kind, source, first[part][0][e])
            pick(0, part, e)
        for part in range(2):
            keep(0, part, e)

    def forward_start():
        for part in range(2):
            y_wait(2 * part + 1, refs["y_out"][part][1], first[part][1][0])
            spread_start(1, part)
        for part in range(2):
            pick(1, part, 0)
            keep(1, part, 0)

    def forward_step(e):
        for part in range(2):
            spread_done(1, part, e)
            pick(1, part, e)
            keep(1, part, e)

    def stand_in(part, hh, send, recv, blocks):
        some = table[part][hh].at[pl.ds(0, blocks)]
        return remote(some, some, send.at[hh, part], recv.at[hh, part], (at(part, 1, 0), h))

    def forward_done(hh):
        for part in range(2):
            stand_in(part, hh, refs["s_send"], refs["s_recv"], 3 * SIDE * SLOT).wait_recv()

    def attention(hh):
        half = slice(hh * HD, (hh + 1) * HD)

        def load_block(b):
            slots = [index[b, j] for j in range(NB)]
            kc = jnp.concatenate([table[0][hh][i] for i in slots], axis=1)
            vc = jnp.concatenate([table[1][hh][i] for i in slots], axis=1)
            q_t = refs["qg"][0][b, half, :].astype(F32) * 0.125
            g_t = refs["qg"][1][b, half, :].astype(F32)
            return kc, vc, q_t, g_t

        def block(i, _):
            blocks = [i * GROUP + n for n in range(GROUP)]
            loaded = [load_block(b) for b in blocks]
            scores = []
            for b, (kc, vc, q_t, g_t) in zip(blocks, loaded):
                s = dot(q_t.T.astype(BF), kc)
                n = count[b]
                scores.append(
                    jnp.concatenate(
                        [
                            jnp.where(j < n, s[:, j * BLK : (j + 1) * BLK], -jnp.inf)
                            for j in range(NB)
                        ],
                        axis=1,
                    )
                )
            probs = []
            for s in scores:
                p = jnp.exp(s - jnp.max(s, axis=1, keepdims=True))
                probs.append(p * (1.0 / jnp.sum(p, axis=1, keepdims=True)))
            lows = [a.astype(BF) for a in probs]
            attns = [dot(low, vc, NT).astype(BF) for low, (_, vc, _, _) in zip(lows, loaded)]
            grads = []
            for a, attn, (kc, vc, q_t, g_t) in zip(probs, attns, loaded):
                g = g_t.T
                delta = jnp.sum(g * attn.astype(F32), axis=1, keepdims=True)
                grads.append((a * (dot(g.astype(BF), vc) - delta)).astype(BF))
            for b, low, ds, attn, (kc, vc, q_t, g_t) in zip(blocks, lows, grads, attns, loaded):
                dq = (dot(ds, kc, NT) * 0.125).astype(BF)
                dk_t = dot(q_t.astype(BF), ds)
                dv_t = dot(g_t.astype(BF), low)
                for j in range(NB):
                    cols = slice(j * BLK, (j + 1) * BLK)
                    terms[0][b * NB + j] = dk_t[:, cols]
                    terms[1][b * NB + j] = dv_t[:, cols]
                if hh == 0:
                    refs["half"][0][b] = attn
                    refs["half"][1][b] = dq
                else:
                    refs["row_out"][0][b] = jnp.concatenate([refs["half"][0][b], attn], axis=1)
                    refs["row_out"][1][b] = jnp.concatenate([refs["half"][1][b], dq], axis=1)
            return 0

        lax.fori_loop(0, NB // GROUP, block, 0)

    def slot_total(part, slot):
        acc = terms[part][index[NB, slot]]
        for b in range(1, NB):
            acc = acc + terms[part][index[NB + b, slot]]
        return acc

    def slot_copy(hh, part, d, e):
        return remote(
            slot_out[part][hh].at[d - 1, e],
            got[part][hh][e].at[pl.ds((d - 1) * SLOT, SLOT)],
            refs["g_send"].at[hh, part], refs["g_recv"].at[hh, part, e],
            (at(part, 0, d), h),
        )

    def backward_start(hh):
        for e in OUTWARD:
            for d in NEAR:
                for part in range(2):

                    def one(r, _, e=e, d=d, part=part):
                        total = slot_total(part, base(part, d, e) + r)
                        slot_out[part][hh][d - 1, e, r] = total.astype(BF)
                        return 0

                    lax.fori_loop(0, SLOT, one, 0)
                    slot_copy(hh, part, d, e).start()
        for part in range(2):
            for e in (1, 2, 3):

                def near(r, _, e=e, part=part):
                    total = slot_total(part, base(part, 0, e) + r)
                    got[part][hh][e][9 + r] = total.astype(BF)
                    return 0

                lax.fori_loop(0, SLOT, near, 0)

            def own(t, _, part=part):
                own_sum[part][hh][t] = slot_total(part, t)
                return 0

            lax.fori_loop(0, NB, own, 0)

    def back_kind(part, e):
        return 18 + 3 * part + e - 1 if e else 9 + 2 * part

    def exchanged(part, e):
        return refs["turned"][part][e - 1] if e else refs["grads"][part][1]

    def back_copy(hh, part, e):
        return remote(
            back_out[part][0].at[e - 1] if hh == 0 else exchanged(part, e),
            back_in[part][hh].at[e - 1],
            refs["b_send"].at[hh, part], refs["b_recv"].at[hh, part],
            (at(part, e, 0), h),
        )

    def backward_turn(e):
        for part in range(2):
            out = final[part][1] if e == 0 else back_out[part][1].at[e - 1]
            y_wait(back_kind(part, e), out, exchanged(part, e))
            if e:
                back_copy(1, part, e).start()

    def backward_step(hh, e):
        for part in range(2):
            some = got[part][hh][e].at[pl.ds(0, 3 * SLOT)]
            remote(
                some, some, refs["g_send"].at[hh, part], refs["g_recv"].at[hh, part, e],
                (at(part, 0, 1), h),
            ).wait_recv()
            source = at(part, e, 0)

            out = final[part][1] if e == 0 else back_out[part][hh].at[e - 1]

            def one(t, _, part=part, source=source, out=out):
                acc = own_sum[part][hh][t] if e == 0 else None
                for d in (0, 1, 2, 3):
                    if d == 0 and e == 0:
                        continue
                    reader = at(part, 0, back_by(d))
                    place = 12
                    for r in range(SLOT):
                        here = (9 if d == 0 else (d - 1) * SLOT) + r
                        place = jnp.where(fetch[r, reader, source] == t, here, place)
                    term = got[part][hh][e][place].astype(F32)
                    acc = term if acc is None else acc + term
                if e == 0 and hh == 0:
                    own_sum[part][hh][t] = acc
                else:
                    out[t] = acc.astype(BF)
                return 0

            lax.fori_loop(0, NB, one, 0)
            if hh == 1:
                y_start(back_kind(part, e), out, exchanged(part, e))
            elif e:
                back_copy(hh, part, e).start()

    def backward_finish():
        for part in range(2):
            stand_in(part, 0, refs["b_send"], refs["b_recv"], 3 * NB).wait_recv()

            def one(t, _, part=part):
                acc = own_sum[part][0][t]
                for e in range(3):
                    acc = acc + back_in[part][0][e, t].astype(F32)
                final[part][0][t] = acc.astype(BF)
                return 0

            lax.fori_loop(0, NB, one, 0)
            y_start(8 + 2 * part, final[part][0], refs["grads"][part][0])

    load_q.wait()
    project(feat, refs["w"][2], NN, put_whole(0))
    forward_second(0)
    forward_first(1)
    forward_first(3)
    forward_start()
    forward_first(2)
    load_gout.wait()
    load_o.wait()
    project(gout, refs["w"][3], NT, put_whole(1))
    y_start(4, refs["qg_out"][0], refs["qg"][0])
    y_start(5, refs["qg_out"][1], refs["qg"][1])
    index_copy.wait()
    forward_second(1)
    forward_second(3)
    forward_second(2)
    for part in range(2):
        terms[part][LIVE] = jnp.zeros((HD, BLK), F32)
        for hh in range(2):
            for e in range(SIDE):
                got[part][hh][e][12] = jnp.zeros((HD, BLK), BF)
    forward_step(1)
    forward_step(3)
    y_wait(4, refs["qg_out"][0], refs["qg"][0])
    y_wait(5, refs["qg_out"][1], refs["qg"][1])
    forward_done(0)
    attention(0)
    forward_step(2)
    backward_start(0)
    forward_done(1)
    attention(1)
    backward_start(1)
    y_start(6, refs["row_out"][0], refs["rows"][0])
    y_start(7, refs["row_out"][1], refs["rows"][1])
    for e in OUTWARD:
        backward_step(0, e)

    def wide(ref):
        return jnp.concatenate([ref[i] for i in range(NB)], axis=1)

    def wide_t(part):
        tiles = []
        for i in range(NB):
            late = refs["grads"][part][1][i].astype(F32)
            for e in range(3):
                late = late + back_in[part][1][e, i].astype(F32)
            tile = jnp.concatenate([refs["grads"][part][0][i].astype(F32), late], axis=0)
            tiles.append(tile.T.astype(BF))
        return jnp.concatenate(tiles, axis=1)

    y_wait(6, refs["row_out"][0], refs["rows"][0])
    refs["att"][...] = dot(wide(refs["rows"][0]), refs["w"][3][...]).astype(BF)
    save_att = load(0, refs["att"], refs["attended"])
    save_att.start()
    y_wait(7, refs["row_out"][1], refs["rows"][1])
    refs["grad"][...] = dot(wide(refs["rows"][1]), refs["w"][2][...], NT)
    for e in OUTWARD:
        backward_step(1, e)
    backward_finish()
    for e in OUTWARD:
        backward_turn(e)
    for part in range(2):
        y_wait(8 + 2 * part, final[part][0], refs["grads"][part][0])
        stand_in(part, 1, refs["b_send"], refs["b_recv"], 3 * NB).wait_recv()
        term = dot(wide_t(part), refs["w"][part][...], NT)
        if part == 0:
            refs["grad"][...] += term
        else:
            refs["gf"][...] = (refs["grad"][...] + term).astype(BF)
    save_gf = load(1, refs["gf"], refs["grad_features"])
    save_gf.start()
    for part in range(2):
        y_all(4 + part, refs["qg_out"][part], refs["qg"][part]).wait_send()
        y_all(6 + part, refs["row_out"][part], refs["rows"][part]).wait_send()
        for hh in range(2):
            y_all(2 * part + hh, refs["y_out"][part][hh], first[part][hh][0]).wait_send()
            y_all(8 + 2 * part + hh, final[part][hh], refs["grads"][part][hh]).wait_send()
            for e in (1, 2, 3):
                if hh == 0:
                    y_all(
                        far_kind(part, e), refs["spread"][part][e - 1], first[part][0][e]
                    ).wait_send()
                else:
                    y_all(
                        back_kind(part, e), back_out[part][1].at[e - 1], exchanged(part, e)
                    ).wait_send()
            for name, blocks in (("f", 24), ("s", 36), ("g", 36), ("b", 24)):
                stand_in(part, hh, refs[name + "_send"], refs["s_recv"], blocks).wait_send()
    save_att.wait()
    save_gf.wait()


def copy_kernel(attended, grad_features, attended_out, grad_features_out):
    attended_out[...] = attended[...]
    grad_features_out[...] = grad_features[...]


def tree_call(layout, kernel):
    flat, tree = jax.tree.flatten(layout, is_leaf=lambda leaf: not isinstance(leaf, (list, dict)))

    def called(names, *refs):
        kernel({**names, **jax.tree.unflatten(tree, refs)})

    return flat, called


def shards(features, grad_out, w_qkv, w_out, kept_slot, kept_count, fetch_slots):
    dma = pltpu.SemaphoreType.DMA
    def vm(*shape, dtype=BF):
        return pltpu.VMEM(shape, dtype)

    def each(make, *counts):
        if not counts:
            return make()
        return [each(make, *counts[1:]) for _ in range(counts[0])]

    tile = (HD, BLK)
    layout = {
        "w": each(lambda: vm(1024, 1024), 4),
        "y_out": each(lambda: vm(NB, *tile), 2, 2),
        "qg_out": each(lambda: vm(NB, BLK, BLK), 2),
        "qg": each(lambda: vm(NB, BLK, BLK), 2),
        "first": each(lambda: vm(NB, *tile), 2, 2, SIDE),
        "spread": each(lambda: vm(NB, *tile), 2, 3),
        "turned": each(lambda: vm(NB, *tile), 2, 3),
        "table": each(lambda: vm(TABLE, *tile), 2, 2),
        "stage": each(lambda: vm(3, SIDE, SLOT, *tile), 2, 2),
        "terms": each(lambda: vm(LIVE + 1, *tile, dtype=F32), 2),
        "half": each(lambda: vm(NB, BLK, HD), 2),
        "row_out": each(lambda: vm(NB, BLK, BLK), 2),
        "rows": each(lambda: vm(NB, BLK, BLK), 2),
        "slot_out": each(lambda: vm(3, SIDE, SLOT, *tile), 2, 2),
        "got": each(lambda: vm(13, *tile), 2, 2, SIDE),
        "own_sum": each(lambda: vm(NB, *tile, dtype=F32), 2, 2),
        "back_out": each(lambda: vm(3, NB, *tile), 2, 2),
        "back_in": each(lambda: vm(3, NB, *tile), 2, 2),
        "final": each(lambda: vm(NB, *tile), 2, 2),
        "grads": each(lambda: vm(NB, *tile), 2, 2),
        "grad": vm(BLK, 1024, dtype=F32),
        "feat": vm(BLK, 1024),
        "gout": vm(BLK, 1024),
        "att": vm(BLK, 1024),
        "gf": vm(BLK, 1024),
        "index_v": vm(2 * NB, BLK, dtype=jnp.int32),
        "index": pltpu.SMEM((2 * NB, BLK), jnp.int32),
        "w_sem": dma((7,)),
        "y_send": dma((24,)),
        "y_recv": dma((24,)),
        "f_send": dma((2, 2)),
        "f_recv": dma((2, 2, 3)),
        "s_send": dma((2, 2)),
        "s_recv": dma((2, 2)),
        "g_send": dma((2, 2)),
        "g_recv": dma((2, 2, SIDE)),
        "b_send": dma((2, 2)),
        "b_recv": dma((2, 2)),
    }
    scratch, called = tree_call(layout, sublayer_kernel)
    names = ("feat_in", "gout_in", "wqkv", "wout", "kept", "count", "fetch")
    names += ("attended", "grad_features")

    def kernel(*refs):
        called(dict(zip(names, refs)), *refs[len(names) :])

    near = pl.BlockSpec(memory_space=pltpu.VMEM)
    far = pl.BlockSpec(memory_space=pl.ANY)
    scalars = pl.BlockSpec(memory_space=pltpu.SMEM)
    out_shape = [jax.ShapeDtypeStruct(features.shape, BF)] * 2
    results = pl.pallas_call(
        kernel,
        out_shape=out_shape,
        in_specs=[far, far, far, far, near, scalars, scalars],
        out_specs=[far, far],
        scratch_shapes=scratch,
        compiler_params=pltpu.CompilerParams(
            collective_id=0, has_side_effects=True, vmem_limit_bytes=VMEM_LIMIT
        ),
    )(
        features, grad_out, w_qkv, w_out, kept_slot, kept_count,
        jnp.transpose(fetch_slots, (2, 0, 1)),
    )
    return pl.pallas_call(
        copy_kernel, out_shape=out_shape, in_specs=[near, near], out_specs=[near, near]
    )(*results)


def solution(mesh):
    rows = P(("cluster", "head"), None)
    in_specs = (rows, rows, P(), P(), P("cluster", None), P("cluster"), P())
    return jax.shard_map(
        shards, mesh=mesh, in_specs=in_specs, out_specs=(rows, rows), check_vma=False
    )
```

```python
import jax
import jax.numpy as jnp
from jax import lax
from jax.experimental import pallas as pl
from jax.experimental.pallas import tpu as pltpu
from jax.sharding import PartitionSpec as P

MESH = pl.DeviceIdType.MESH
BF = jnp.bfloat16
F32 = jnp.float32
BLK = 128
HD = 64
NB = 8
SIDE = 4
SLOT = 3
TABLE = NB + SIDE * SIDE * SLOT
GROUP = 4
LIVE = NB * NB
NEAR = (1, 3, 2)
OUTWARD = (2, 1, 3, 0)
VMEM_LIMIT = 56 << 20

NN = (((1,), (0,)), ((), ()))
NT = (((1,), (1,)), ((), ()))


def dot(a, b, dims=NN):
    return lax.dot_general(a, b, dims, preferred_element_type=F32)


def back_by(d):
    return (SIDE - d) % SIDE


def base(part, d, e):
    return NB + ((e * SIDE + d) if part == 0 else (d * SIDE + e)) * SLOT


def sublayer_kernel(refs):
    feat, gout, wqkv, wout = refs["feat"], refs["gout"], refs["wqkv"], refs["wout"]
    index, count, fetch = refs["index"], refs["count"], refs["fetch"]
    first, table, stage = refs["first"], refs["table"], refs["stage"]
    terms, slot_out, got = refs["terms"], refs["slot_out"], refs["got"]
    own_sum, back_out, back_in = refs["own_sum"], refs["back_out"], refs["back_in"]
    final = refs["final"]
    c = lax.axis_index("cluster")
    h = lax.axis_index("head")
    x, z = c // SIDE, c % SIDE

    def at(part, a, b):
        if part == 1:
            a, b = b, a
        return lax.rem(x + a, SIDE) * SIDE + lax.rem(z + b, SIDE)

    def load(n, src, dst):
        return pltpu.make_async_copy(src, dst, refs["w_sem"].at[n])

    loads = [load(4, refs["feat_in"], feat), load(5, refs["gout_in"], gout)]
    for n, piece in enumerate((1, 2, 0)):
        loads.append(load(n, wqkv.at[:, pl.ds(piece * 1024, 1024)], refs["w"][n]))
    loads.append(load(3, wout, refs["w"][3]))
    load_feat, load_gout, load_k, load_v, load_q, load_o = loads
    load_feat.start()
    load_k.start()
    load_v.start()

    barrier = pltpu.get_barrier_semaphore()
    for d in (1, 2, 3):
        for part in range(2):
            pl.semaphore_signal(
                barrier, inc=1, device_id=(at(part, d, 0), h), device_id_type=MESH
            )
    for d in range(1, NB):
        pl.semaphore_signal(
            barrier, inc=1, device_id=(c, lax.rem(h + d, NB)), device_id_type=MESH
        )

    def remote(src, dst, send, recv, device):
        return pltpu.make_async_remote_copy(
            src, dst, send, recv, device_id=device, device_id_type=MESH
        )

    def y_copy(kind, src, dst, peer):
        return remote(src, dst, refs["y_send"].at[kind], refs["y_recv"].at[kind], (c, peer))

    def y_start(kind, src, dest):
        for d in range(1, NB):
            to = lax.rem(h + d, NB)
            y_copy(kind, src.at[to], dest.at[h], to).start()
        dest[h] = src[h]

    def y_all(kind, src, dest):
        others = pl.ds(0, NB - 1)
        return y_copy(kind, src.at[others], dest.at[others], lax.rem(h + 1, NB))

    def y_wait(kind, src, dest):
        y_all(kind, src, dest).wait_recv()

    def project(rows, weight, dims, put):
        for p in range(4):
            if dims is NN:
                w = weight[:, p * 256 : (p + 1) * 256]
            else:
                w = weight[p * 256 : (p + 1) * 256, :]
            out = dot(rows[...], w, dims)
            put(2 * p, out[:, :BLK].T.astype(BF))
            put(2 * p + 1, out[:, BLK:].T.astype(BF))

    def put_heads(outs):
        def put(dest, tile):
            outs[0][dest] = tile[:HD]
            outs[1][dest] = tile[HD:]

        return put

    def qg_kind(n, hh):
        return 24 + n if hh else 4 + n

    def qg_start(hh):
        for n in range(2):
            y_start(qg_kind(n, hh), refs["qg_out"][n][hh], refs["qg"][n][hh])

    def row_kind(n, hh):
        return 26 + n if hh else 6 + n

    def rows_start(hh):
        for n in range(2):
            y_start(row_kind(n, hh), refs["row_out"][n][hh], refs["rows"][n][hh])

    def rows_wait(n):
        for hh in range(2):
            y_wait(row_kind(n, hh), refs["row_out"][n][hh], refs["rows"][n][hh])

    def qg_wait(hh):
        for n in range(2):
            y_wait(qg_kind(n, hh), refs["qg_out"][n][hh], refs["qg"][n][hh])

    def index_tables():
        kept = refs["kept"][...]
        fetched = jnp.maximum(kept - NB, 0)
        source = (fetched * 43) >> 7
        e = ((source >> 2) - x + SIDE) & 3
        f = ((source & 3) - z + SIDE) & 3
        relative = NB + (e * SIDE + f) * SLOT + fetched - source * SLOT
        slots = jnp.where(kept < NB, kept, relative)
        row = lax.broadcasted_iota(jnp.int32, (NB, NB), 0)
        limit = jnp.zeros((NB, NB), jnp.int32)
        for b in range(NB):
            limit = jnp.where(row == b, count[b], limit)
        column = lax.broadcasted_iota(jnp.int32, (NB, NB), 1)
        slots = jnp.where(column < limit, slots, row)
        lane = lax.broadcasted_iota(jnp.int32, (NB, BLK), 1)
        wide_row = lax.broadcasted_iota(jnp.int32, (NB, BLK), 0)
        entry_of = jnp.full((NB, BLK), LIVE, jnp.int32)
        for j in range(NB):
            hit = (slots[:, j : j + 1] == lane) & (limit[:, j : j + 1] > j)
            entry_of = jnp.where(hit, wide_row * NB + j, entry_of)
        refs["index_v"][0:NB] = jnp.zeros((NB, BLK), jnp.int32)
        refs["index_v"][0:NB, 0:NB] = slots
        refs["index_v"][NB : 2 * NB] = entry_of
        copy = load(6, refs["index_v"], index)
        copy.start()
        return copy

    def spread_copy(hh, part, src, e, blocks, to):
        if hh == 0:
            source = refs["spread"][part][src - 1] if src else refs["y_out"][part][0]
            target = refs["spread"][part][e - 1]
        else:
            source, target = first[part][1][src], first[part][1][e]
        return remote(
            source.at[blocks], target.at[blocks],
            refs["f_send"].at[hh, part], refs["f_recv"].at[hh, part, e - 1],
            (at(part, to, 0), h),
        )

    def spread_start(hh, part):
        for e in (1, 3):
            spread_copy(hh, part, 0, e, pl.ds(0, NB), back_by(e)).start()

    def spread_done(hh, part, e):
        spread_copy(hh, part, 0, e, pl.ds(0, NB), e).wait_recv()
        spread_relay(hh, part, e)

    def spread_relay(hh, part, e):
        if e == 1:
            spread_copy(hh, part, 1, 2, pl.ds(0, NB // 2), 3).start()
        if e == 3:
            spread_copy(hh, part, 3, 2, pl.ds(NB // 2, NB // 2), 1).start()

    index_copy = index_tables()
    load_feat.wait()
    load_k.wait()
    project(feat, refs["w"][0], NN, put_heads(refs["y_out"][0]))
    pl.semaphore_wait(barrier, 6 + NB - 1)
    spread_start(0, 0)
    y_start(0, refs["y_out"][0][0], first[0][0][0])
    load_gout.start()
    load_q.start()
    load_o.start()
    load_v.wait()
    project(feat, refs["w"][1], NN, put_heads(refs["y_out"][1]))
    spread_start(0, 1)
    y_start(2, refs["y_out"][1][0], first[1][0][0])
    y_start(1, refs["y_out"][0][1], first[0][1][0])
    y_start(3, refs["y_out"][1][1], first[1][1][0])
    def pick_copy(hh, part, d, e):
        return remote(
            stage[part][hh].at[d - 1, e],
            table[part][hh].at[pl.ds(base(part, d, e), SLOT)],
            refs["s_send"].at[hh, part], refs["s_recv"].at[hh, part],
            (at(part, 0, back_by(d)), h),
        )

    def pick(hh, part, e):
        source = at(part, e, 0)
        for d in NEAR:
            reader = at(part, 0, back_by(d))
            for r in range(SLOT):
                stage[part][hh][d - 1, e, r] = first[part][hh][e][fetch[r, reader, source]]
            pick_copy(hh, part, d, e).start()

    def keep(hh, part, e):
        if e == 0:
            for t in range(NB):
                table[part][hh][t] = first[part][hh][0][t]
        else:
            source = at(part, e, 0)
            for r in range(SLOT):
                table[part][hh][base(part, 0, e) + r] = first[part][hh][e][fetch[r, c, source]]

    def far_kind(part, e):
        return 12 + 3 * part + e - 1

    def forward_first(e):
        for part in range(2):
            spread_done(0, part, e)
            y_start(far_kind(part, e), refs["spread"][part][e - 1], first[part][0][e])

    def forward_second(e):
        for part in range(2):
            kind = far_kind(part, e) if e else 2 * part
            source = refs["spread"][part][e - 1] if e else refs["y_out"][part][0]
            y_wait(kind, source, first[part][0][e])
            pick(0, part, e)
        for part in range(2):
            keep(0, part, e)

    def forward_start():
        for part in range(2):
            y_wait(2 * part + 1, refs["y_out"][part][1], first[part][1][0])
            spread_start(1, part)
        for part in range(2):
            pick(1, part, 0)
            keep(1, part, 0)

    def forward_relay(e):
        for part in range(2):
            spread_done(1, part, e)

    def forward_step(e):
        for part in range(2):
            if e == 2:
                spread_done(1, part, e)
            pick(1, part, e)
            keep(1, part, e)

    def stand_in(part, hh, send, recv, blocks):
        some = table[part][hh].at[pl.ds(0, blocks)]
        return remote(some, some, send.at[hh, part], recv.at[hh, part], (at(part, 1, 0), h))

    def forward_done(hh):
        for part in range(2):
            stand_in(part, hh, refs["s_send"], refs["s_recv"], 3 * SIDE * SLOT).wait_recv()

    def attention(hh):
        def load_block(b):
            slots = [index[b, j] for j in range(NB)]
            kc = jnp.concatenate([table[0][hh][i] for i in slots], axis=1)
            vc = jnp.concatenate([table[1][hh][i] for i in slots], axis=1)
            q_t = refs["qg"][0][hh][b].astype(F32) * 0.125
            g_t = refs["qg"][1][hh][b].astype(F32)
            return kc, vc, q_t, g_t

        def block(i, _):
            blocks = [i * GROUP + n for n in range(GROUP)]
            loaded = [load_block(b) for b in blocks]
            scores = []
            for b, (kc, vc, q_t, g_t) in zip(blocks, loaded):
                s = dot(q_t.T.astype(BF), kc)
                n = count[b]
                scores.append(
                    jnp.concatenate(
                        [
                            jnp.where(j < n, s[:, j * BLK : (j + 1) * BLK], -jnp.inf)
                            for j in range(NB)
                        ],
                        axis=1,
                    )
                )
            probs = []
            for s in scores:
                p = jnp.exp(s - jnp.max(s, axis=1, keepdims=True))
                probs.append(p * (1.0 / jnp.sum(p, axis=1, keepdims=True)))
            lows = [a.astype(BF) for a in probs]
            attns = [dot(low, vc, NT).astype(BF) for low, (_, vc, _, _) in zip(lows, loaded)]
            grads = []
            for a, attn, (kc, vc, q_t, g_t) in zip(probs, attns, loaded):
                g = g_t.T
                delta = jnp.sum(g * attn.astype(F32), axis=1, keepdims=True)
                grads.append((a * (dot(g.astype(BF), vc) - delta)).astype(BF))
            for b, low, ds, attn, (kc, vc, q_t, g_t) in zip(blocks, lows, grads, attns, loaded):
                dq = dot(ds, kc, NT) * 0.125
                dk_t = dot(q_t.astype(BF), ds)
                dv_t = dot(g_t.astype(BF), low)
                for j in range(NB):
                    cols = slice(j * BLK, (j + 1) * BLK)
                    terms[0][b * NB + j] = dk_t[:, cols]
                    terms[1][b * NB + j] = dv_t[:, cols]
                refs["row_out"][0][hh][b] = attn.astype(F32).T.astype(BF)
                refs["row_out"][1][hh][b] = dq.T.astype(BF)
            return 0

        lax.fori_loop(0, NB // GROUP, block, 0)

    def slot_total(part, slot):
        acc = terms[part][index[NB, slot]]
        for b in range(1, NB):
            acc = acc + terms[part][index[NB + b, slot]]
        return acc

    def slot_copy(hh, part, d, e):
        return remote(
            slot_out[part][hh].at[d - 1, e],
            got[part][hh][e].at[pl.ds((d - 1) * SLOT, SLOT)],
            refs["g_send"].at[hh, part], refs["g_recv"].at[hh, part, e],
            (at(part, 0, d), h),
        )

    def backward_start(hh):
        for e in OUTWARD:
            for d in NEAR:
                for part in range(2):

                    def one(r, _, e=e, d=d, part=part):
                        total = slot_total(part, base(part, d, e) + r)
                        slot_out[part][hh][d - 1, e, r] = total.astype(BF)
                        return 0

                    lax.fori_loop(0, SLOT, one, 0)
                    slot_copy(hh, part, d, e).start()
        for part in range(2):
            for e in (1, 2, 3):

                def near(r, _, e=e, part=part):
                    total = slot_total(part, base(part, 0, e) + r)
                    got[part][hh][e][9 + r] = total.astype(BF)
                    return 0

                lax.fori_loop(0, SLOT, near, 0)

            def own(t, _, part=part):
                own_sum[part][hh][t] = slot_total(part, t)
                return 0

            lax.fori_loop(0, NB, own, 0)

    def back_kind(part, e):
        return 18 + 3 * part + e - 1 if e else 9 + 2 * part

    def exchanged(part, e):
        return refs["turned"][part][e - 1] if e else refs["grads"][part][1]

    def back_copy(hh, part, e):
        return remote(
            back_out[part][0].at[e - 1] if hh == 0 else exchanged(part, e),
            back_in[part][hh].at[e - 1],
            refs["b_send"].at[hh, part], refs["b_recv"].at[hh, part],
            (at(part, e, 0), h),
        )

    def backward_turn(e):
        for part in range(2):
            out = final[part][1] if e == 0 else back_out[part][1].at[e - 1]
            y_wait(back_kind(part, e), out, exchanged(part, e))
            if e:
                back_copy(1, part, e).start()

    def backward_step(hh, e):
        for part in range(2):
            some = got[part][hh][e].at[pl.ds(0, 3 * SLOT)]
            remote(
                some, some, refs["g_send"].at[hh, part], refs["g_recv"].at[hh, part, e],
                (at(part, 0, 1), h),
            ).wait_recv()
            source = at(part, e, 0)

            out = final[part][1] if e == 0 else back_out[part][hh].at[e - 1]

            def one(t, _, part=part, source=source, out=out):
                acc = own_sum[part][hh][t] if e == 0 else None
                for d in (0, 1, 2, 3):
                    if d == 0 and e == 0:
                        continue
                    reader = at(part, 0, back_by(d))
                    place = 12
                    for r in range(SLOT):
                        here = (9 if d == 0 else (d - 1) * SLOT) + r
                        place = jnp.where(fetch[r, reader, source] == t, here, place)
                    term = got[part][hh][e][place].astype(F32)
                    acc = term if acc is None else acc + term
                if e == 0 and hh == 0:
                    own_sum[part][hh][t] = acc
                else:
                    out[t] = acc.astype(BF)
                return 0

            lax.fori_loop(0, NB, one, 0)
            if hh == 1:
                y_start(back_kind(part, e), out, exchanged(part, e))
            elif e:
                back_copy(hh, part, e).start()

    def backward_finish():
        for part in range(2):
            stand_in(part, 0, refs["b_send"], refs["b_recv"], 3 * NB).wait_recv()

            def one(t, _, part=part):
                acc = own_sum[part][0][t]
                for e in range(3):
                    acc = acc + back_in[part][0][e, t].astype(F32)
                final[part][0][t] = acc.astype(BF)
                return 0

            lax.fori_loop(0, NB, one, 0)
            y_start(8 + 2 * part, final[part][0], refs["grads"][part][0])

    load_q.wait()
    project(feat, refs["w"][2], NN, put_heads(refs["qg_out"][0]))
    forward_second(0)
    forward_first(1)
    forward_first(3)
    forward_start()
    forward_first(2)
    load_gout.wait()
    load_o.wait()
    project(gout, refs["w"][3], NT, put_heads(refs["qg_out"][1]))
    qg_start(0)
    qg_start(1)
    index_copy.wait()
    forward_second(1)
    forward_second(3)
    forward_relay(1)
    forward_relay(3)
    forward_second(2)
    for part in range(2):
        terms[part][LIVE] = jnp.zeros((HD, BLK), F32)
        for hh in range(2):
            for e in range(SIDE):
                got[part][hh][e][12] = jnp.zeros((HD, BLK), BF)
    for e in NEAR:
        forward_step(e)
    qg_wait(0)
    forward_done(0)
    attention(0)
    rows_start(0)
    backward_start(0)
    forward_done(1)
    qg_wait(1)
    attention(1)
    backward_start(1)
    rows_start(1)
    for e in OUTWARD:
        backward_step(0, e)

    def wide_rows(n):
        tiles = []
        for i in range(NB):
            tile = jnp.concatenate([refs["rows"][n][hh][i] for hh in range(2)], axis=0)
            tiles.append(tile.astype(F32).T.astype(BF))
        return jnp.concatenate(tiles, axis=1)

    def wide_t(part):
        tiles = []
        for i in range(NB):
            late = refs["grads"][part][1][i].astype(F32)
            for e in range(3):
                late = late + back_in[part][1][e, i].astype(F32)
            tile = jnp.concatenate([refs["grads"][part][0][i].astype(F32), late], axis=0)
            tiles.append(tile.T.astype(BF))
        return jnp.concatenate(tiles, axis=1)

    backward_step(1, 2)
    rows_wait(0)
    refs["att"][...] = dot(wide_rows(0), refs["w"][3][...]).astype(BF)
    save_att = load(0, refs["att"], refs["attended"])
    save_att.start()
    backward_step(1, 1)
    rows_wait(1)
    refs["grad"][...] = dot(wide_rows(1), refs["w"][2][...], NT)
    backward_step(1, 3)
    backward_turn(2)
    backward_step(1, 0)
    backward_turn(1)
    backward_turn(3)
    backward_finish()
    backward_turn(0)
    for part in range(2):
        y_wait(8 + 2 * part, final[part][0], refs["grads"][part][0])
        stand_in(part, 1, refs["b_send"], refs["b_recv"], 3 * NB).wait_recv()
        term = dot(wide_t(part), refs["w"][part][...], NT)
        if part == 0:
            refs["grad"][...] += term
        else:
            refs["gf"][...] = (refs["grad"][...] + term).astype(BF)
    save_gf = load(1, refs["gf"], refs["grad_features"])
    save_gf.start()
    for part in range(2):
        for hh in range(2):
            y_all(qg_kind(part, hh), refs["qg_out"][part][hh], refs["qg"][part][hh]).wait_send()
            y_all(row_kind(part, hh), refs["row_out"][part][hh], refs["rows"][part][hh]).wait_send()
        for hh in range(2):
            y_all(2 * part + hh, refs["y_out"][part][hh], first[part][hh][0]).wait_send()
            y_all(8 + 2 * part + hh, final[part][hh], refs["grads"][part][hh]).wait_send()
            for e in (1, 2, 3):
                if hh == 0:
                    y_all(
                        far_kind(part, e), refs["spread"][part][e - 1], first[part][0][e]
                    ).wait_send()
                else:
                    y_all(
                        back_kind(part, e), back_out[part][1].at[e - 1], exchanged(part, e)
                    ).wait_send()
            for name, blocks in (("f", 24), ("s", 36), ("g", 36), ("b", 24)):
                stand_in(part, hh, refs[name + "_send"], refs["s_recv"], blocks).wait_send()
    save_att.wait()
    save_gf.wait()


def copy_kernel(attended, grad_features, attended_out, grad_features_out):
    attended_out[...] = attended[...]
    grad_features_out[...] = grad_features[...]


def tree_call(layout, kernel):
    flat, tree = jax.tree.flatten(layout, is_leaf=lambda leaf: not isinstance(leaf, (list, dict)))

    def called(names, *refs):
        kernel({**names, **jax.tree.unflatten(tree, refs)})

    return flat, called


def shards(features, grad_out, w_qkv, w_out, kept_slot, kept_count, fetch_slots):
    dma = pltpu.SemaphoreType.DMA
    def vm(*shape, dtype=BF):
        return pltpu.VMEM(shape, dtype)

    def each(make, *counts):
        if not counts:
            return make()
        return [each(make, *counts[1:]) for _ in range(counts[0])]

    tile = (HD, BLK)
    layout = {
        "w": each(lambda: vm(1024, 1024), 4),
        "y_out": each(lambda: vm(NB, *tile), 2, 2),
        "qg_out": each(lambda: vm(NB, *tile), 2, 2),
        "qg": each(lambda: vm(NB, *tile), 2, 2),
        "first": each(lambda: vm(NB, *tile), 2, 2, SIDE),
        "spread": each(lambda: vm(NB, *tile), 2, 3),
        "turned": each(lambda: vm(NB, *tile), 2, 3),
        "table": each(lambda: vm(TABLE, *tile), 2, 2),
        "stage": each(lambda: vm(3, SIDE, SLOT, *tile), 2, 2),
        "terms": each(lambda: vm(LIVE + 1, *tile, dtype=F32), 2),
        "row_out": each(lambda: vm(NB, *tile), 2, 2),
        "rows": each(lambda: vm(NB, *tile), 2, 2),
        "slot_out": each(lambda: vm(3, SIDE, SLOT, *tile), 2, 2),
        "got": each(lambda: vm(13, *tile), 2, 2, SIDE),
        "own_sum": each(lambda: vm(NB, *tile, dtype=F32), 2, 2),
        "back_out": each(lambda: vm(3, NB, *tile), 2, 2),
        "back_in": each(lambda: vm(3, NB, *tile), 2, 2),
        "final": each(lambda: vm(NB, *tile), 2, 2),
        "grads": each(lambda: vm(NB, *tile), 2, 2),
        "grad": vm(BLK, 1024, dtype=F32),
        "feat": vm(BLK, 1024),
        "gout": vm(BLK, 1024),
        "att": vm(BLK, 1024),
        "gf": vm(BLK, 1024),
        "index_v": vm(2 * NB, BLK, dtype=jnp.int32),
        "index": pltpu.SMEM((2 * NB, BLK), jnp.int32),
        "w_sem": dma((7,)),
        "y_send": dma((28,)),
        "y_recv": dma((28,)),
        "f_send": dma((2, 2)),
        "f_recv": dma((2, 2, 3)),
        "s_send": dma((2, 2)),
        "s_recv": dma((2, 2)),
        "g_send": dma((2, 2)),
        "g_recv": dma((2, 2, SIDE)),
        "b_send": dma((2, 2)),
        "b_recv": dma((2, 2)),
    }
    scratch, called = tree_call(layout, sublayer_kernel)
    names = ("feat_in", "gout_in", "wqkv", "wout", "kept", "count", "fetch")
    names += ("attended", "grad_features")

    def kernel(*refs):
        called(dict(zip(names, refs)), *refs[len(names) :])

    near = pl.BlockSpec(memory_space=pltpu.VMEM)
    far = pl.BlockSpec(memory_space=pl.ANY)
    scalars = pl.BlockSpec(memory_space=pltpu.SMEM)
    out_shape = [jax.ShapeDtypeStruct(features.shape, BF)] * 2
    results = pl.pallas_call(
        kernel,
        out_shape=out_shape,
        in_specs=[far, far, far, far, near, scalars, scalars],
        out_specs=[far, far],
        scratch_shapes=scratch,
        compiler_params=pltpu.CompilerParams(
            collective_id=0, has_side_effects=True, vmem_limit_bytes=VMEM_LIMIT
        ),
    )(
        features, grad_out, w_qkv, w_out, kept_slot, kept_count,
        jnp.transpose(fetch_slots, (2, 0, 1)),
    )
    return pl.pallas_call(
        copy_kernel, out_shape=out_shape, in_specs=[near, near], out_specs=[near, near]
    )(*results)


def solution(mesh):
    rows = P(("cluster", "head"), None)
    in_specs = (rows, rows, P(), P(), P("cluster", None), P("cluster"), P())
    return jax.shard_map(
        shards, mesh=mesh, in_specs=in_specs, out_specs=(rows, rows), check_vma=False
    )
```

```python
import jax
import jax.numpy as jnp
from jax import lax
from jax.experimental import pallas as pl
from jax.experimental.pallas import tpu as pltpu
from jax.sharding import PartitionSpec as P

MESH = pl.DeviceIdType.MESH
BF = jnp.bfloat16
F32 = jnp.float32
BLK = 128
HD = 64
NB = 8
SIDE = 4
SLOT = 3
TABLE = NB + SIDE * SIDE * SLOT
GROUP = 4
LIVE = NB * NB
NEAR = (1, 3, 2)
OUTWARD = (2, 1, 3, 0)
VMEM_LIMIT = 56 << 20

NN = (((1,), (0,)), ((), ()))
NT = (((1,), (1,)), ((), ()))


def dot(a, b, dims=NN):
    return lax.dot_general(a, b, dims, preferred_element_type=F32)


def back_by(d):
    return (SIDE - d) % SIDE


def base(part, d, e):
    return NB + ((e * SIDE + d) if part == 0 else (d * SIDE + e)) * SLOT


def sublayer_kernel(refs):
    feat, gout, wqkv, wout = refs["feat"], refs["gout"], refs["wqkv"], refs["wout"]
    index, count, fetch = refs["index"], refs["count"], refs["fetch"]
    first, table, stage = refs["first"], refs["table"], refs["stage"]
    terms, slot_out, got = refs["terms"], refs["slot_out"], refs["got"]
    own_sum, back_out, back_in = refs["own_sum"], refs["back_out"], refs["back_in"]
    final = refs["final"]
    c = lax.axis_index("cluster")
    h = lax.axis_index("head")
    x, z = c // SIDE, c % SIDE

    def at(part, a, b):
        if part == 1:
            a, b = b, a
        return lax.rem(x + a, SIDE) * SIDE + lax.rem(z + b, SIDE)

    def load(n, src, dst):
        return pltpu.make_async_copy(src, dst, refs["w_sem"].at[n])

    loads = [load(4, refs["feat_in"], feat), load(5, refs["gout_in"], gout)]
    for n, piece in enumerate((1, 2, 0)):
        loads.append(load(n, wqkv.at[:, pl.ds(piece * 1024, 1024)], refs["w"][n]))
    loads.append(load(3, wout, refs["w"][3]))
    load_feat, load_gout, load_k, load_v, load_q, load_o = loads
    load_feat.start()
    load_k.start()
    load_v.start()

    barrier = pltpu.get_barrier_semaphore()
    for d in (1, 2, 3):
        for part in range(2):
            pl.semaphore_signal(
                barrier, inc=1, device_id=(at(part, d, 0), h), device_id_type=MESH
            )
    for d in range(1, NB):
        pl.semaphore_signal(
            barrier, inc=1, device_id=(c, lax.rem(h + d, NB)), device_id_type=MESH
        )

    def remote(src, dst, send, recv, device):
        return pltpu.make_async_remote_copy(
            src, dst, send, recv, device_id=device, device_id_type=MESH
        )

    def y_copy(kind, src, dst, peer):
        return remote(src, dst, refs["y_send"].at[kind], refs["y_recv"].at[kind], (c, peer))

    def y_start(kind, src, dest):
        for d in range(1, NB):
            to = lax.rem(h + d, NB)
            y_copy(kind, src.at[to], dest.at[h], to).start()
        dest[h] = src[h]

    def y_all(kind, src, dest):
        others = pl.ds(0, NB - 1)
        return y_copy(kind, src.at[others], dest.at[others], lax.rem(h + 1, NB))

    def y_wait(kind, src, dest):
        y_all(kind, src, dest).wait_recv()

    def project(rows, weight, dims, put):
        for p in range(4):
            if dims is NN:
                w = weight[:, p * 256 : (p + 1) * 256]
            else:
                w = weight[p * 256 : (p + 1) * 256, :]
            out = dot(rows[...], w, dims)
            put(2 * p, out[:, :BLK].T.astype(BF))
            put(2 * p + 1, out[:, BLK:].T.astype(BF))

    def put_heads(outs):
        def put(dest, tile):
            outs[0][dest] = tile[:HD]
            outs[1][dest] = tile[HD:]

        return put

    def qg_kind(n, hh):
        return 24 + n if hh else 4 + n

    def qg_start(hh):
        for n in range(2):
            y_start(qg_kind(n, hh), refs["qg_out"][n][hh], refs["qg"][n][hh])

    def row_kind(n, hh):
        return 26 + n if hh else 6 + n

    def rows_start(hh):
        for n in range(2):
            y_start(row_kind(n, hh), refs["row_out"][n][hh], refs["rows"][n][hh])

    def rows_wait(n):
        for hh in range(2):
            y_wait(row_kind(n, hh), refs["row_out"][n][hh], refs["rows"][n][hh])

    def qg_wait(hh):
        for n in range(2):
            y_wait(qg_kind(n, hh), refs["qg_out"][n][hh], refs["qg"][n][hh])

    def index_tables():
        kept = refs["kept"][...]
        fetched = jnp.maximum(kept - NB, 0)
        source = (fetched * 43) >> 7
        e = ((source >> 2) - x + SIDE) & 3
        f = ((source & 3) - z + SIDE) & 3
        relative = NB + (e * SIDE + f) * SLOT + fetched - source * SLOT
        slots = jnp.where(kept < NB, kept, relative)
        row = lax.broadcasted_iota(jnp.int32, (NB, NB), 0)
        limit = jnp.zeros((NB, NB), jnp.int32)
        for b in range(NB):
            limit = jnp.where(row == b, count[b], limit)
        column = lax.broadcasted_iota(jnp.int32, (NB, NB), 1)
        slots = jnp.where(column < limit, slots, row)
        lane = lax.broadcasted_iota(jnp.int32, (NB, BLK), 1)
        wide_row = lax.broadcasted_iota(jnp.int32, (NB, BLK), 0)
        entry_of = jnp.full((NB, BLK), LIVE, jnp.int32)
        for j in range(NB):
            hit = (slots[:, j : j + 1] == lane) & (limit[:, j : j + 1] > j)
            entry_of = jnp.where(hit, wide_row * NB + j, entry_of)
        refs["index_v"][0:NB] = jnp.zeros((NB, BLK), jnp.int32)
        refs["index_v"][0:NB, 0:NB] = slots
        refs["index_v"][NB : 2 * NB] = entry_of
        copy = load(6, refs["index_v"], index)
        copy.start()
        return copy

    def spread_copy(hh, part, src, e, blocks, to):
        if hh == 0:
            source = refs["spread"][part][src - 1] if src else refs["y_out"][part][0]
            target = refs["spread"][part][e - 1]
        else:
            source, target = first[part][1][src], first[part][1][e]
        return remote(
            source.at[blocks], target.at[blocks],
            refs["f_send"].at[hh, part], refs["f_recv"].at[hh, part, e - 1],
            (at(part, to, 0), h),
        )

    def spread_start(hh, part):
        for e in NEAR if hh == 0 else (1, 3):
            spread_copy(hh, part, 0, e, pl.ds(0, NB), back_by(e)).start()

    def spread_done(hh, part, e):
        spread_copy(hh, part, 0, e, pl.ds(0, NB), e).wait_recv()
        spread_relay(hh, part, e)

    def spread_relay(hh, part, e):
        if hh == 0:
            return
        if e == 1:
            spread_copy(hh, part, 1, 2, pl.ds(0, NB // 2), 3).start()
        if e == 3:
            spread_copy(hh, part, 3, 2, pl.ds(NB // 2, NB // 2), 1).start()

    index_copy = index_tables()
    load_feat.wait()
    load_k.wait()
    project(feat, refs["w"][0], NN, put_heads(refs["y_out"][0]))
    pl.semaphore_wait(barrier, 6 + NB - 1)
    spread_start(0, 0)
    y_start(0, refs["y_out"][0][0], first[0][0][0])
    load_gout.start()
    load_q.start()
    load_o.start()
    load_v.wait()
    project(feat, refs["w"][1], NN, put_heads(refs["y_out"][1]))
    spread_start(0, 1)
    y_start(2, refs["y_out"][1][0], first[1][0][0])
    y_start(1, refs["y_out"][0][1], first[0][1][0])
    y_start(3, refs["y_out"][1][1], first[1][1][0])
    def pick_copy(hh, part, d, e):
        return remote(
            stage[part][hh].at[d - 1, e],
            table[part][hh].at[pl.ds(base(part, d, e), SLOT)],
            refs["s_send"].at[hh, part], refs["s_recv"].at[hh, part],
            (at(part, 0, back_by(d)), h),
        )

    def pick(hh, part, e):
        source = at(part, e, 0)
        for d in NEAR:
            reader = at(part, 0, back_by(d))
            for r in range(SLOT):
                stage[part][hh][d - 1, e, r] = first[part][hh][e][fetch[r, reader, source]]
            pick_copy(hh, part, d, e).start()

    def keep(hh, part, e):
        if e == 0:
            for t in range(NB):
                table[part][hh][t] = first[part][hh][0][t]
        else:
            source = at(part, e, 0)
            for r in range(SLOT):
                table[part][hh][base(part, 0, e) + r] = first[part][hh][e][fetch[r, c, source]]

    def far_kind(part, e):
        return 12 + 3 * part + e - 1

    def forward_first(e):
        for part in range(2):
            spread_done(0, part, e)
            y_start(far_kind(part, e), refs["spread"][part][e - 1], first[part][0][e])

    def forward_second(e):
        for part in range(2):
            kind = far_kind(part, e) if e else 2 * part
            source = refs["spread"][part][e - 1] if e else refs["y_out"][part][0]
            y_wait(kind, source, first[part][0][e])
            pick(0, part, e)
        for part in range(2):
            keep(0, part, e)

    def forward_start():
        for part in range(2):
            y_wait(2 * part + 1, refs["y_out"][part][1], first[part][1][0])
            spread_start(1, part)
        for part in range(2):
            pick(1, part, 0)
            keep(1, part, 0)

    def forward_relay(e):
        for part in range(2):
            spread_done(1, part, e)

    def forward_step(e):
        for part in range(2):
            if e == 2:
                spread_done(1, part, e)
            pick(1, part, e)
            keep(1, part, e)

    def stand_in(part, hh, send, recv, blocks):
        some = table[part][hh].at[pl.ds(0, blocks)]
        return remote(some, some, send.at[hh, part], recv.at[hh, part], (at(part, 1, 0), h))

    def forward_done(hh):
        for part in range(2):
            stand_in(part, hh, refs["s_send"], refs["s_recv"], 3 * SIDE * SLOT).wait_recv()

    def attention(hh):
        def load_block(b):
            slots = [index[b, j] for j in range(NB)]
            kc = jnp.concatenate([table[0][hh][i] for i in slots], axis=1)
            vc = jnp.concatenate([table[1][hh][i] for i in slots], axis=1)
            q_t = refs["qg"][0][hh][b].astype(F32) * 0.125
            g_t = refs["qg"][1][hh][b].astype(F32)
            return kc, vc, q_t, g_t

        def block(i, _):
            blocks = [i * GROUP + n for n in range(GROUP)]
            loaded = [load_block(b) for b in blocks]
            scores = []
            for b, (kc, vc, q_t, g_t) in zip(blocks, loaded):
                s = dot(q_t.T.astype(BF), kc)
                n = count[b]
                scores.append(
                    jnp.concatenate(
                        [
                            jnp.where(j < n, s[:, j * BLK : (j + 1) * BLK], -jnp.inf)
                            for j in range(NB)
                        ],
                        axis=1,
                    )
                )
            probs = []
            for s in scores:
                p = jnp.exp(s - jnp.max(s, axis=1, keepdims=True))
                probs.append(p * (1.0 / jnp.sum(p, axis=1, keepdims=True)))
            lows = [a.astype(BF) for a in probs]
            attns = [dot(low, vc, NT).astype(BF) for low, (_, vc, _, _) in zip(lows, loaded)]
            grads = []
            for a, attn, (kc, vc, q_t, g_t) in zip(probs, attns, loaded):
                g = g_t.T
                delta = jnp.sum(g * attn.astype(F32), axis=1, keepdims=True)
                grads.append((a * (dot(g.astype(BF), vc) - delta)).astype(BF))
            for b, low, ds, attn, (kc, vc, q_t, g_t) in zip(blocks, lows, grads, attns, loaded):
                dq = dot(ds, kc, NT) * 0.125
                dk_t = dot(q_t.astype(BF), ds)
                dv_t = dot(g_t.astype(BF), low)
                for j in range(NB):
                    cols = slice(j * BLK, (j + 1) * BLK)
                    terms[0][b * NB + j] = dk_t[:, cols]
                    terms[1][b * NB + j] = dv_t[:, cols]
                refs["row_out"][0][hh][b] = attn.astype(F32).T.astype(BF)
                refs["row_out"][1][hh][b] = dq.T.astype(BF)
            return 0

        lax.fori_loop(0, NB // GROUP, block, 0)

    def slot_total(part, slot):
        acc = terms[part][index[NB, slot]]
        for b in range(1, NB):
            acc = acc + terms[part][index[NB + b, slot]]
        return acc

    def slot_copy(hh, part, d, e):
        return remote(
            slot_out[part][hh].at[d - 1, e],
            got[part][hh][e].at[pl.ds((d - 1) * SLOT, SLOT)],
            refs["g_send"].at[hh, part], refs["g_recv"].at[hh, part, e],
            (at(part, 0, d), h),
        )

    def backward_start(hh):
        for e in OUTWARD:
            for d in NEAR:
                for part in range(2):

                    def one(r, _, e=e, d=d, part=part):
                        total = slot_total(part, base(part, d, e) + r)
                        slot_out[part][hh][d - 1, e, r] = total.astype(BF)
                        return 0

                    lax.fori_loop(0, SLOT, one, 0)
                    slot_copy(hh, part, d, e).start()
        for part in range(2):
            for e in (1, 2, 3):

                def near(r, _, e=e, part=part):
                    total = slot_total(part, base(part, 0, e) + r)
                    got[part][hh][e][9 + r] = total.astype(BF)
                    return 0

                lax.fori_loop(0, SLOT, near, 0)

            def own(t, _, part=part):
                own_sum[part][hh][t] = slot_total(part, t)
                return 0

            lax.fori_loop(0, NB, own, 0)

    def back_kind(part, e):
        return 18 + 3 * part + e - 1 if e else 9 + 2 * part

    def exchanged(part, e):
        return refs["turned"][part][e - 1] if e else refs["grads"][part][1]

    def back_copy(hh, part, e):
        return remote(
            back_out[part][0].at[e - 1] if hh == 0 else exchanged(part, e),
            back_in[part][hh].at[e - 1],
            refs["b_send"].at[hh, part], refs["b_recv"].at[hh, part],
            (at(part, e, 0), h),
        )

    def backward_turn(e):
        for part in range(2):
            out = final[part][1] if e == 0 else back_out[part][1].at[e - 1]
            y_wait(back_kind(part, e), out, exchanged(part, e))
            if e:
                back_copy(1, part, e).start()

    def backward_step(hh, e):
        for part in range(2):
            some = got[part][hh][e].at[pl.ds(0, 3 * SLOT)]
            remote(
                some, some, refs["g_send"].at[hh, part], refs["g_recv"].at[hh, part, e],
                (at(part, 0, 1), h),
            ).wait_recv()
            source = at(part, e, 0)

            out = final[part][1] if e == 0 else back_out[part][hh].at[e - 1]

            def one(t, _, part=part, source=source, out=out):
                acc = own_sum[part][hh][t] if e == 0 else None
                for d in (0, 1, 2, 3):
                    if d == 0 and e == 0:
                        continue
                    reader = at(part, 0, back_by(d))
                    place = 12
                    for r in range(SLOT):
                        here = (9 if d == 0 else (d - 1) * SLOT) + r
                        place = jnp.where(fetch[r, reader, source] == t, here, place)
                    term = got[part][hh][e][place].astype(F32)
                    acc = term if acc is None else acc + term
                if e == 0 and hh == 0:
                    own_sum[part][hh][t] = acc
                else:
                    out[t] = acc.astype(BF)
                return 0

            lax.fori_loop(0, NB, one, 0)
            if hh == 1:
                y_start(back_kind(part, e), out, exchanged(part, e))
            elif e:
                back_copy(hh, part, e).start()

    def backward_finish():
        for part in range(2):
            stand_in(part, 0, refs["b_send"], refs["b_recv"], 3 * NB).wait_recv()

            def one(t, _, part=part):
                acc = own_sum[part][0][t]
                for e in range(3):
                    acc = acc + back_in[part][0][e, t].astype(F32)
                final[part][0][t] = acc.astype(BF)
                return 0

            lax.fori_loop(0, NB, one, 0)
            y_start(8 + 2 * part, final[part][0], refs["grads"][part][0])

    load_q.wait()
    project(feat, refs["w"][2], NN, put_heads(refs["qg_out"][0]))
    forward_second(0)
    forward_first(1)
    forward_first(3)
    forward_start()
    forward_first(2)
    load_gout.wait()
    load_o.wait()
    project(gout, refs["w"][3], NT, put_heads(refs["qg_out"][1]))
    qg_start(0)
    qg_start(1)
    index_copy.wait()
    forward_second(1)
    forward_second(3)
    forward_relay(1)
    forward_relay(3)
    forward_second(2)
    for part in range(2):
        terms[part][LIVE] = jnp.zeros((HD, BLK), F32)
        for hh in range(2):
            for e in range(SIDE):
                got[part][hh][e][12] = jnp.zeros((HD, BLK), BF)
    for e in NEAR:
        forward_step(e)
    qg_wait(0)
    forward_done(0)
    attention(0)
    rows_start(0)
    backward_start(0)
    forward_done(1)
    qg_wait(1)
    attention(1)
    backward_start(1)
    rows_start(1)
    for e in OUTWARD:
        backward_step(0, e)

    def wide_rows(n):
        tiles = []
        for i in range(NB):
            tile = jnp.concatenate([refs["rows"][n][hh][i] for hh in range(2)], axis=0)
            tiles.append(tile.astype(F32).T.astype(BF))
        return jnp.concatenate(tiles, axis=1)

    def wide_t(part):
        tiles = []
        for i in range(NB):
            late = refs["grads"][part][1][i].astype(F32)
            for e in range(3):
                late = late + back_in[part][1][e, i].astype(F32)
            tile = jnp.concatenate([refs["grads"][part][0][i].astype(F32), late], axis=0)
            tiles.append(tile.T.astype(BF))
        return jnp.concatenate(tiles, axis=1)

    backward_step(1, 2)
    rows_wait(0)
    refs["att"][...] = dot(wide_rows(0), refs["w"][3][...]).astype(BF)
    save_att = load(0, refs["att"], refs["attended"])
    save_att.start()
    backward_step(1, 1)
    rows_wait(1)
    refs["grad"][...] = dot(wide_rows(1), refs["w"][2][...], NT)
    backward_step(1, 3)
    backward_turn(2)
    backward_step(1, 0)
    backward_turn(1)
    backward_turn(3)
    backward_finish()
    backward_turn(0)
    for part in range(2):
        y_wait(8 + 2 * part, final[part][0], refs["grads"][part][0])
        stand_in(part, 1, refs["b_send"], refs["b_recv"], 3 * NB).wait_recv()
        term = dot(wide_t(part), refs["w"][part][...], NT)
        if part == 0:
            refs["grad"][...] += term
        else:
            refs["gf"][...] = (refs["grad"][...] + term).astype(BF)
    save_gf = load(1, refs["gf"], refs["grad_features"])
    save_gf.start()
    for part in range(2):
        for hh in range(2):
            y_all(qg_kind(part, hh), refs["qg_out"][part][hh], refs["qg"][part][hh]).wait_send()
            y_all(row_kind(part, hh), refs["row_out"][part][hh], refs["rows"][part][hh]).wait_send()
        for hh in range(2):
            y_all(2 * part + hh, refs["y_out"][part][hh], first[part][hh][0]).wait_send()
            y_all(8 + 2 * part + hh, final[part][hh], refs["grads"][part][hh]).wait_send()
            for e in (1, 2, 3):
                if hh == 0:
                    y_all(
                        far_kind(part, e), refs["spread"][part][e - 1], first[part][0][e]
                    ).wait_send()
                else:
                    y_all(
                        back_kind(part, e), back_out[part][1].at[e - 1], exchanged(part, e)
                    ).wait_send()
            for name, blocks in (("f", 24), ("s", 36), ("g", 36), ("b", 24)):
                stand_in(part, hh, refs[name + "_send"], refs["s_recv"], blocks).wait_send()
    save_att.wait()
    save_gf.wait()


def copy_kernel(attended, grad_features, attended_out, grad_features_out):
    attended_out[...] = attended[...]
    grad_features_out[...] = grad_features[...]


def tree_call(layout, kernel):
    flat, tree = jax.tree.flatten(layout, is_leaf=lambda leaf: not isinstance(leaf, (list, dict)))

    def called(names, *refs):
        kernel({**names, **jax.tree.unflatten(tree, refs)})

    return flat, called


def shards(features, grad_out, w_qkv, w_out, kept_slot, kept_count, fetch_slots):
    dma = pltpu.SemaphoreType.DMA
    def vm(*shape, dtype=BF):
        return pltpu.VMEM(shape, dtype)

    def each(make, *counts):
        if not counts:
            return make()
        return [each(make, *counts[1:]) for _ in range(counts[0])]

    tile = (HD, BLK)
    layout = {
        "w": each(lambda: vm(1024, 1024), 4),
        "y_out": each(lambda: vm(NB, *tile), 2, 2),
        "qg_out": each(lambda: vm(NB, *tile), 2, 2),
        "qg": each(lambda: vm(NB, *tile), 2, 2),
        "first": each(lambda: vm(NB, *tile), 2, 2, SIDE),
        "spread": each(lambda: vm(NB, *tile), 2, 3),
        "turned": each(lambda: vm(NB, *tile), 2, 3),
        "table": each(lambda: vm(TABLE, *tile), 2, 2),
        "stage": each(lambda: vm(3, SIDE, SLOT, *tile), 2, 2),
        "terms": each(lambda: vm(LIVE + 1, *tile, dtype=F32), 2),
        "row_out": each(lambda: vm(NB, *tile), 2, 2),
        "rows": each(lambda: vm(NB, *tile), 2, 2),
        "slot_out": each(lambda: vm(3, SIDE, SLOT, *tile), 2, 2),
        "got": each(lambda: vm(13, *tile), 2, 2, SIDE),
        "own_sum": each(lambda: vm(NB, *tile, dtype=F32), 2, 2),
        "back_out": each(lambda: vm(3, NB, *tile), 2, 2),
        "back_in": each(lambda: vm(3, NB, *tile), 2, 2),
        "final": each(lambda: vm(NB, *tile), 2, 2),
        "grads": each(lambda: vm(NB, *tile), 2, 2),
        "grad": vm(BLK, 1024, dtype=F32),
        "feat": vm(BLK, 1024),
        "gout": vm(BLK, 1024),
        "att": vm(BLK, 1024),
        "gf": vm(BLK, 1024),
        "index_v": vm(2 * NB, BLK, dtype=jnp.int32),
        "index": pltpu.SMEM((2 * NB, BLK), jnp.int32),
        "w_sem": dma((7,)),
        "y_send": dma((28,)),
        "y_recv": dma((28,)),
        "f_send": dma((2, 2)),
        "f_recv": dma((2, 2, 3)),
        "s_send": dma((2, 2)),
        "s_recv": dma((2, 2)),
        "g_send": dma((2, 2)),
        "g_recv": dma((2, 2, SIDE)),
        "b_send": dma((2, 2)),
        "b_recv": dma((2, 2)),
    }
    scratch, called = tree_call(layout, sublayer_kernel)
    names = ("feat_in", "gout_in", "wqkv", "wout", "kept", "count", "fetch")
    names += ("attended", "grad_features")

    def kernel(*refs):
        called(dict(zip(names, refs)), *refs[len(names) :])

    near = pl.BlockSpec(memory_space=pltpu.VMEM)
    far = pl.BlockSpec(memory_space=pl.ANY)
    scalars = pl.BlockSpec(memory_space=pltpu.SMEM)
    out_shape = [jax.ShapeDtypeStruct(features.shape, BF)] * 2
    results = pl.pallas_call(
        kernel,
        out_shape=out_shape,
        in_specs=[far, far, far, far, near, scalars, scalars],
        out_specs=[far, far],
        scratch_shapes=scratch,
        compiler_params=pltpu.CompilerParams(
            collective_id=0, has_side_effects=True, vmem_limit_bytes=VMEM_LIMIT
        ),
    )(
        features, grad_out, w_qkv, w_out, kept_slot, kept_count,
        jnp.transpose(fetch_slots, (2, 0, 1)),
    )
    return pl.pallas_call(
        copy_kernel, out_shape=out_shape, in_specs=[near, near], out_specs=[near, near]
    )(*results)


def solution(mesh):
    rows = P(("cluster", "head"), None)
    in_specs = (rows, rows, P(), P(), P("cluster", None), P("cluster"), P())
    return jax.shard_map(
        shards, mesh=mesh, in_specs=in_specs, out_specs=(rows, rows), check_vma=False
    )
```

```python
import jax
import jax.numpy as jnp
from jax import lax
from jax.experimental import pallas as pl
from jax.experimental.pallas import tpu as pltpu
from jax.sharding import PartitionSpec as P

MESH = pl.DeviceIdType.MESH
BF = jnp.bfloat16
F32 = jnp.float32
BLK = 128
HD = 64
NB = 8
SIDE = 4
SLOT = 3
TABLE = NB + SIDE * SIDE * SLOT
GROUP = 4
LIVE = NB * NB
NEAR = (1, 3, 2)
OUTWARD = (2, 1, 3, 0)
VMEM_LIMIT = 56 << 20

NN = (((1,), (0,)), ((), ()))
NT = (((1,), (1,)), ((), ()))


def dot(a, b, dims=NN):
    return lax.dot_general(a, b, dims, preferred_element_type=F32)


def back_by(d):
    return (SIDE - d) % SIDE


def base(part, d, e):
    return NB + ((e * SIDE + d) if part == 0 else (d * SIDE + e)) * SLOT


def sublayer_kernel(refs):
    feat, gout, wqkv, wout = refs["feat"], refs["gout"], refs["wqkv"], refs["wout"]
    index, count, fetch = refs["index"], refs["count"], refs["fetch"]
    first, table, stage = refs["first"], refs["table"], refs["stage"]
    terms, slot_out, got = refs["terms"], refs["slot_out"], refs["got"]
    own_sum, back_out, back_in = refs["own_sum"], refs["back_out"], refs["back_in"]
    final = refs["final"]
    c = lax.axis_index("cluster")
    h = lax.axis_index("head")
    x, z = c // SIDE, c % SIDE

    def at(part, a, b):
        if part == 1:
            a, b = b, a
        return lax.rem(x + a, SIDE) * SIDE + lax.rem(z + b, SIDE)

    def load(n, src, dst):
        return pltpu.make_async_copy(src, dst, refs["w_sem"].at[n])

    loads = [load(4, refs["feat_in"], feat), load(5, refs["gout_in"], gout)]
    for n, piece in enumerate((1, 2, 0)):
        loads.append(load(n, wqkv.at[:, pl.ds(piece * 1024, 1024)], refs["w"][n]))
    loads.append(load(3, wout, refs["w"][3]))
    load_feat, load_gout, load_k, load_v, load_q, load_o = loads
    load_feat.start()
    load_k.start()

    barrier = pltpu.get_barrier_semaphore()
    for d in (1, 2, 3):
        for part in range(2):
            pl.semaphore_signal(
                barrier, inc=1, device_id=(at(part, d, 0), h), device_id_type=MESH
            )
    for d in range(1, NB):
        pl.semaphore_signal(
            barrier, inc=1, device_id=(c, lax.rem(h + d, NB)), device_id_type=MESH
        )

    def remote(src, dst, send, recv, device):
        return pltpu.make_async_remote_copy(
            src, dst, send, recv, device_id=device, device_id_type=MESH
        )

    def y_copy(kind, src, dst, peer):
        return remote(src, dst, refs["y_send"].at[kind], refs["y_recv"].at[kind], (c, peer))

    def y_start(kind, src, dest):
        for d in range(1, NB):
            to = lax.rem(h + d, NB)
            y_copy(kind, src.at[to], dest.at[h], to).start()
        dest[h] = src[h]

    def y_all(kind, src, dest):
        others = pl.ds(0, NB - 1)
        return y_copy(kind, src.at[others], dest.at[others], lax.rem(h + 1, NB))

    def y_wait(kind, src, dest):
        y_all(kind, src, dest).wait_recv()

    def project(rows, weight, dims, put):
        for p in range(4):
            if dims is NN:
                w = weight[:, p * 256 : (p + 1) * 256]
            else:
                w = weight[p * 256 : (p + 1) * 256, :]
            out = dot(rows[...], w, dims)
            put(2 * p, out[:, :BLK].T.astype(BF))
            put(2 * p + 1, out[:, BLK:].T.astype(BF))

    def put_heads(outs):
        def put(dest, tile):
            outs[0][dest] = tile[:HD]
            outs[1][dest] = tile[HD:]

        return put

    def qg_kind(n, hh):
        return 24 + n if hh else 4 + n

    def qg_start(hh):
        for n in range(2):
            y_start(qg_kind(n, hh), refs["qg_out"][n][hh], refs["qg"][n][hh])

    def row_kind(n, hh):
        return 26 + n if hh else 6 + n

    def rows_start(hh):
        for n in range(2):
            y_start(row_kind(n, hh), refs["row_out"][n][hh], refs["rows"][n][hh])

    def rows_wait(n):
        for hh in range(2):
            y_wait(row_kind(n, hh), refs["row_out"][n][hh], refs["rows"][n][hh])

    def qg_wait(hh):
        for n in range(2):
            y_wait(qg_kind(n, hh), refs["qg_out"][n][hh], refs["qg"][n][hh])

    def index_tables():
        kept = refs["kept"][...]
        fetched = jnp.maximum(kept - NB, 0)
        source = (fetched * 43) >> 7
        e = ((source >> 2) - x + SIDE) & 3
        f = ((source & 3) - z + SIDE) & 3
        relative = NB + (e * SIDE + f) * SLOT + fetched - source * SLOT
        slots = jnp.where(kept < NB, kept, relative)
        row = lax.broadcasted_iota(jnp.int32, (NB, NB), 0)
        limit = jnp.zeros((NB, NB), jnp.int32)
        for b in range(NB):
            limit = jnp.where(row == b, count[b], limit)
        column = lax.broadcasted_iota(jnp.int32, (NB, NB), 1)
        slots = jnp.where(column < limit, slots, row)
        lane = lax.broadcasted_iota(jnp.int32, (NB, BLK), 1)
        wide_row = lax.broadcasted_iota(jnp.int32, (NB, BLK), 0)
        entry_of = jnp.full((NB, BLK), LIVE, jnp.int32)
        for j in range(NB):
            hit = (slots[:, j : j + 1] == lane) & (limit[:, j : j + 1] > j)
            entry_of = jnp.where(hit, wide_row * NB + j, entry_of)
        refs["index_v"][0:NB] = jnp.zeros((NB, BLK), jnp.int32)
        refs["index_v"][0:NB, 0:NB] = slots
        refs["index_v"][NB : 2 * NB] = entry_of
        copy = load(6, refs["index_v"], index)
        copy.start()
        return copy

    def spread_copy(hh, part, src, e, blocks, to):
        if hh == 0:
            source = refs["spread"][part][src - 1] if src else refs["y_out"][part][0]
            target = refs["spread"][part][e - 1]
        else:
            source, target = first[part][1][src], first[part][1][e]
        return remote(
            source.at[blocks], target.at[blocks],
            refs["f_send"].at[hh, part], refs["f_recv"].at[hh, part, e - 1],
            (at(part, to, 0), h),
        )

    def spread_start(hh, part):
        for e in NEAR if hh == 0 else (1, 3):
            spread_copy(hh, part, 0, e, pl.ds(0, NB), back_by(e)).start()

    def spread_done(hh, part, e):
        spread_copy(hh, part, 0, e, pl.ds(0, NB), e).wait_recv()
        spread_relay(hh, part, e)

    def spread_relay(hh, part, e):
        if hh == 0:
            return
        if e == 1:
            spread_copy(hh, part, 1, 2, pl.ds(0, NB // 2), 3).start()
        if e == 3:
            spread_copy(hh, part, 3, 2, pl.ds(NB // 2, NB // 2), 1).start()

    load_feat.wait()
    load_k.wait()
    load_v.start()
    project(feat, refs["w"][0], NN, put_heads(refs["y_out"][0]))
    pl.semaphore_wait(barrier, 6 + NB - 1)
    spread_start(0, 0)
    y_start(0, refs["y_out"][0][0], first[0][0][0])
    load_gout.start()
    load_q.start()
    load_o.start()
    load_v.wait()
    project(feat, refs["w"][1], NN, put_heads(refs["y_out"][1]))
    spread_start(0, 1)
    y_start(2, refs["y_out"][1][0], first[1][0][0])
    y_start(1, refs["y_out"][0][1], first[0][1][0])
    y_start(3, refs["y_out"][1][1], first[1][1][0])
    index_copy = index_tables()
    def pick_copy(hh, part, d, e):
        return remote(
            stage[part][hh].at[d - 1, e],
            table[part][hh].at[pl.ds(base(part, d, e), SLOT)],
            refs["s_send"].at[hh, part], refs["s_recv"].at[hh, part],
            (at(part, 0, back_by(d)), h),
        )

    def pick(hh, part, e):
        source = at(part, e, 0)
        for d in NEAR:
            reader = at(part, 0, back_by(d))
            for r in range(SLOT):
                stage[part][hh][d - 1, e, r] = first[part][hh][e][fetch[r, reader, source]]
            pick_copy(hh, part, d, e).start()

    def keep(hh, part, e):
        if e == 0:
            for t in range(NB):
                table[part][hh][t] = first[part][hh][0][t]
        else:
            source = at(part, e, 0)
            for r in range(SLOT):
                table[part][hh][base(part, 0, e) + r] = first[part][hh][e][fetch[r, c, source]]

    def far_kind(part, e):
        return 12 + 3 * part + e - 1

    def forward_first(e):
        for part in range(2):
            spread_done(0, part, e)
            y_start(far_kind(part, e), refs["spread"][part][e - 1], first[part][0][e])

    def forward_second(e):
        for part in range(2):
            kind = far_kind(part, e) if e else 2 * part
            source = refs["spread"][part][e - 1] if e else refs["y_out"][part][0]
            y_wait(kind, source, first[part][0][e])
            pick(0, part, e)
        for part in range(2):
            keep(0, part, e)

    def forward_start():
        for part in range(2):
            y_wait(2 * part + 1, refs["y_out"][part][1], first[part][1][0])
            spread_start(1, part)
        for part in range(2):
            pick(1, part, 0)
            keep(1, part, 0)

    def forward_relay(e):
        for part in range(2):
            spread_done(1, part, e)

    def forward_step(e):
        for part in range(2):
            if e == 2:
                spread_done(1, part, e)
            pick(1, part, e)
            keep(1, part, e)

    def stand_in(part, hh, send, recv, blocks):
        some = table[part][hh].at[pl.ds(0, blocks)]
        return remote(some, some, send.at[hh, part], recv.at[hh, part], (at(part, 1, 0), h))

    def forward_done(hh):
        for part in range(2):
            stand_in(part, hh, refs["s_send"], refs["s_recv"], 3 * SIDE * SLOT).wait_recv()

    def attention(hh):
        def load_block(b):
            slots = [index[b, j] for j in range(NB)]
            kc = jnp.concatenate([table[0][hh][i] for i in slots], axis=1)
            vc = jnp.concatenate([table[1][hh][i] for i in slots], axis=1)
            q_t = refs["qg"][0][hh][b].astype(F32) * 0.125
            g_t = refs["qg"][1][hh][b].astype(F32)
            return kc, vc, q_t, g_t

        def block(i, _):
            blocks = [i * GROUP + n for n in range(GROUP)]
            loaded = [load_block(b) for b in blocks]
            scores = []
            for b, (kc, vc, q_t, g_t) in zip(blocks, loaded):
                s = dot(q_t.T.astype(BF), kc)
                n = count[b]
                scores.append(
                    jnp.concatenate(
                        [
                            jnp.where(j < n, s[:, j * BLK : (j + 1) * BLK], -jnp.inf)
                            for j in range(NB)
                        ],
                        axis=1,
                    )
                )
            probs = []
            for s in scores:
                p = jnp.exp(s - jnp.max(s, axis=1, keepdims=True))
                probs.append(p * (1.0 / jnp.sum(p, axis=1, keepdims=True)))
            lows = [a.astype(BF) for a in probs]
            attns = [dot(low, vc, NT).astype(BF) for low, (_, vc, _, _) in zip(lows, loaded)]
            grads = []
            for a, attn, (kc, vc, q_t, g_t) in zip(probs, attns, loaded):
                g = g_t.T
                delta = jnp.sum(g * attn.astype(F32), axis=1, keepdims=True)
                grads.append((a * (dot(g.astype(BF), vc) - delta)).astype(BF))
            for b, low, ds, attn, (kc, vc, q_t, g_t) in zip(blocks, lows, grads, attns, loaded):
                dq = dot(ds, kc, NT) * 0.125
                dk_t = dot(q_t.astype(BF), ds)
                dv_t = dot(g_t.astype(BF), low)
                for j in range(NB):
                    cols = slice(j * BLK, (j + 1) * BLK)
                    terms[0][b * NB + j] = dk_t[:, cols]
                    terms[1][b * NB + j] = dv_t[:, cols]
                refs["row_out"][0][hh][b] = attn.astype(F32).T.astype(BF)
                refs["row_out"][1][hh][b] = dq.T.astype(BF)
            return 0

        lax.fori_loop(0, NB // GROUP, block, 0)

    def slot_total(part, slot):
        acc = terms[part][index[NB, slot]]
        for b in range(1, NB):
            acc = acc + terms[part][index[NB + b, slot]]
        return acc

    def slot_copy(hh, part, d, e):
        return remote(
            slot_out[part][hh].at[d - 1, e],
            got[part][hh][e].at[pl.ds((d - 1) * SLOT, SLOT)],
            refs["g_send"].at[hh, part], refs["g_recv"].at[hh, part, e],
            (at(part, 0, d), h),
        )

    def backward_start(hh):
        for e in OUTWARD:
            for d in NEAR:
                for part in range(2):

                    def one(r, _, e=e, d=d, part=part):
                        total = slot_total(part, base(part, d, e) + r)
                        slot_out[part][hh][d - 1, e, r] = total.astype(BF)
                        return 0

                    lax.fori_loop(0, SLOT, one, 0)
                    slot_copy(hh, part, d, e).start()
        for part in range(2):
            for e in (1, 2, 3):

                def near(r, _, e=e, part=part):
                    total = slot_total(part, base(part, 0, e) + r)
                    got[part][hh][e][9 + r] = total.astype(BF)
                    return 0

                lax.fori_loop(0, SLOT, near, 0)

            def own(t, _, part=part):
                own_sum[part][hh][t] = slot_total(part, t)
                return 0

            lax.fori_loop(0, NB, own, 0)

    def back_kind(part, e):
        return 18 + 3 * part + e - 1 if e else 9 + 2 * part

    def exchanged(part, e):
        return refs["turned"][part][e - 1] if e else refs["grads"][part][1]

    def back_copy(hh, part, e):
        return remote(
            back_out[part][0].at[e - 1] if hh == 0 else exchanged(part, e),
            back_in[part][hh].at[e - 1],
            refs["b_send"].at[hh, part], refs["b_recv"].at[hh, part],
            (at(part, e, 0), h),
        )

    def backward_turn(e):
        for part in range(2):
            out = final[part][1] if e == 0 else back_out[part][1].at[e - 1]
            y_wait(back_kind(part, e), out, exchanged(part, e))
            if e:
                back_copy(1, part, e).start()

    def backward_step(hh, e):
        for part in range(2):
            some = got[part][hh][e].at[pl.ds(0, 3 * SLOT)]
            remote(
                some, some, refs["g_send"].at[hh, part], refs["g_recv"].at[hh, part, e],
                (at(part, 0, 1), h),
            ).wait_recv()
            source = at(part, e, 0)

            out = final[part][1] if e == 0 else back_out[part][hh].at[e - 1]

            def one(t, _, part=part, source=source, out=out):
                acc = own_sum[part][hh][t] if e == 0 else None
                for d in (0, 1, 2, 3):
                    if d == 0 and e == 0:
                        continue
                    reader = at(part, 0, back_by(d))
                    place = 12
                    for r in range(SLOT):
                        here = (9 if d == 0 else (d - 1) * SLOT) + r
                        place = jnp.where(fetch[r, reader, source] == t, here, place)
                    term = got[part][hh][e][place].astype(F32)
                    acc = term if acc is None else acc + term
                if e == 0 and hh == 0:
                    own_sum[part][hh][t] = acc
                else:
                    out[t] = acc.astype(BF)
                return 0

            lax.fori_loop(0, NB, one, 0)
            if hh == 1:
                y_start(back_kind(part, e), out, exchanged(part, e))
            elif e:
                back_copy(hh, part, e).start()

    def backward_finish():
        for part in range(2):
            stand_in(part, 0, refs["b_send"], refs["b_recv"], 3 * NB).wait_recv()

            def one(t, _, part=part):
                acc = own_sum[part][0][t]
                for e in range(3):
                    acc = acc + back_in[part][0][e, t].astype(F32)
                final[part][0][t] = acc.astype(BF)
                return 0

            lax.fori_loop(0, NB, one, 0)
            y_start(8 + 2 * part, final[part][0], refs["grads"][part][0])

    load_q.wait()
    project(feat, refs["w"][2], NN, put_heads(refs["qg_out"][0]))
    forward_second(0)
    forward_first(1)
    forward_first(3)
    forward_start()
    forward_first(2)
    load_gout.wait()
    load_o.wait()
    project(gout, refs["w"][3], NT, put_heads(refs["qg_out"][1]))
    qg_start(0)
    qg_start(1)
    index_copy.wait()
    forward_second(1)
    forward_relay(1)
    forward_relay(3)
    forward_second(3)
    forward_second(2)
    for part in range(2):
        terms[part][LIVE] = jnp.zeros((HD, BLK), F32)
        for hh in range(2):
            for e in range(SIDE):
                got[part][hh][e][12] = jnp.zeros((HD, BLK), BF)
    for e in NEAR:
        forward_step(e)
    qg_wait(0)
    forward_done(0)
    attention(0)
    rows_start(0)
    backward_start(0)
    forward_done(1)
    qg_wait(1)
    attention(1)
    backward_start(1)
    rows_start(1)
    for e in OUTWARD:
        backward_step(0, e)

    def wide_rows(n):
        tiles = []
        for i in range(NB):
            tile = jnp.concatenate([refs["rows"][n][hh][i] for hh in range(2)], axis=0)
            tiles.append(tile.astype(F32).T.astype(BF))
        return jnp.concatenate(tiles, axis=1)

    def wide_t(part):
        tiles = []
        for i in range(NB):
            late = refs["grads"][part][1][i].astype(F32)
            for e in range(3):
                late = late + back_in[part][1][e, i].astype(F32)
            tile = jnp.concatenate([refs["grads"][part][0][i].astype(F32), late], axis=0)
            tiles.append(tile.T.astype(BF))
        return jnp.concatenate(tiles, axis=1)

    backward_step(1, 2)
    rows_wait(0)
    refs["att"][...] = dot(wide_rows(0), refs["w"][3][...]).astype(BF)
    save_att = load(0, refs["att"], refs["attended"])
    save_att.start()
    backward_step(1, 1)
    rows_wait(1)
    refs["grad"][...] = dot(wide_rows(1), refs["w"][2][...], NT)
    backward_step(1, 3)
    backward_turn(2)
    backward_step(1, 0)
    backward_turn(1)
    backward_turn(3)
    backward_finish()
    backward_turn(0)
    for part in range(2):
        y_wait(8 + 2 * part, final[part][0], refs["grads"][part][0])
        stand_in(part, 1, refs["b_send"], refs["b_recv"], 3 * NB).wait_recv()
        term = dot(wide_t(part), refs["w"][part][...], NT)
        if part == 0:
            refs["grad"][...] += term
        else:
            refs["gf"][...] = (refs["grad"][...] + term).astype(BF)
    save_gf = load(1, refs["gf"], refs["grad_features"])
    save_gf.start()
    for part in range(2):
        for hh in range(2):
            y_all(qg_kind(part, hh), refs["qg_out"][part][hh], refs["qg"][part][hh]).wait_send()
            y_all(row_kind(part, hh), refs["row_out"][part][hh], refs["rows"][part][hh]).wait_send()
        for hh in range(2):
            y_all(2 * part + hh, refs["y_out"][part][hh], first[part][hh][0]).wait_send()
            y_all(8 + 2 * part + hh, final[part][hh], refs["grads"][part][hh]).wait_send()
            for e in (1, 2, 3):
                if hh == 0:
                    y_all(
                        far_kind(part, e), refs["spread"][part][e - 1], first[part][0][e]
                    ).wait_send()
                else:
                    y_all(
                        back_kind(part, e), back_out[part][1].at[e - 1], exchanged(part, e)
                    ).wait_send()
            for name, blocks in (("f", 24), ("s", 36), ("g", 36), ("b", 24)):
                stand_in(part, hh, refs[name + "_send"], refs["s_recv"], blocks).wait_send()
    save_att.wait()
    save_gf.wait()


def copy_kernel(attended, grad_features, attended_out, grad_features_out):
    attended_out[...] = attended[...]
    grad_features_out[...] = grad_features[...]


def tree_call(layout, kernel):
    flat, tree = jax.tree.flatten(layout, is_leaf=lambda leaf: not isinstance(leaf, (list, dict)))

    def called(names, *refs):
        kernel({**names, **jax.tree.unflatten(tree, refs)})

    return flat, called


def shards(features, grad_out, w_qkv, w_out, kept_slot, kept_count, fetch_slots):
    dma = pltpu.SemaphoreType.DMA
    def vm(*shape, dtype=BF):
        return pltpu.VMEM(shape, dtype)

    def each(make, *counts):
        if not counts:
            return make()
        return [each(make, *counts[1:]) for _ in range(counts[0])]

    tile = (HD, BLK)
    layout = {
        "w": each(lambda: vm(1024, 1024), 4),
        "y_out": each(lambda: vm(NB, *tile), 2, 2),
        "qg_out": each(lambda: vm(NB, *tile), 2, 2),
        "qg": each(lambda: vm(NB, *tile), 2, 2),
        "first": each(lambda: vm(NB, *tile), 2, 2, SIDE),
        "spread": each(lambda: vm(NB, *tile), 2, 3),
        "turned": each(lambda: vm(NB, *tile), 2, 3),
        "table": each(lambda: vm(TABLE, *tile), 2, 2),
        "stage": each(lambda: vm(3, SIDE, SLOT, *tile), 2, 2),
        "terms": each(lambda: vm(LIVE + 1, *tile, dtype=F32), 2),
        "row_out": each(lambda: vm(NB, *tile), 2, 2),
        "rows": each(lambda: vm(NB, *tile), 2, 2),
        "slot_out": each(lambda: vm(3, SIDE, SLOT, *tile), 2, 2),
        "got": each(lambda: vm(13, *tile), 2, 2, SIDE),
        "own_sum": each(lambda: vm(NB, *tile, dtype=F32), 2, 2),
        "back_out": each(lambda: vm(3, NB, *tile), 2, 2),
        "back_in": each(lambda: vm(3, NB, *tile), 2, 2),
        "final": each(lambda: vm(NB, *tile), 2, 2),
        "grads": each(lambda: vm(NB, *tile), 2, 2),
        "grad": vm(BLK, 1024, dtype=F32),
        "feat": vm(BLK, 1024),
        "gout": vm(BLK, 1024),
        "att": vm(BLK, 1024),
        "gf": vm(BLK, 1024),
        "index_v": vm(2 * NB, BLK, dtype=jnp.int32),
        "index": pltpu.SMEM((2 * NB, BLK), jnp.int32),
        "w_sem": dma((7,)),
        "y_send": dma((28,)),
        "y_recv": dma((28,)),
        "f_send": dma((2, 2)),
        "f_recv": dma((2, 2, 3)),
        "s_send": dma((2, 2)),
        "s_recv": dma((2, 2)),
        "g_send": dma((2, 2)),
        "g_recv": dma((2, 2, SIDE)),
        "b_send": dma((2, 2)),
        "b_recv": dma((2, 2)),
    }
    scratch, called = tree_call(layout, sublayer_kernel)
    names = ("feat_in", "gout_in", "wqkv", "wout", "kept", "count", "fetch")
    names += ("attended", "grad_features")

    def kernel(*refs):
        called(dict(zip(names, refs)), *refs[len(names) :])

    near = pl.BlockSpec(memory_space=pltpu.VMEM)
    far = pl.BlockSpec(memory_space=pl.ANY)
    scalars = pl.BlockSpec(memory_space=pltpu.SMEM)
    out_shape = [jax.ShapeDtypeStruct(features.shape, BF)] * 2
    results = pl.pallas_call(
        kernel,
        out_shape=out_shape,
        in_specs=[far, far, far, far, near, scalars, scalars],
        out_specs=[far, far],
        scratch_shapes=scratch,
        compiler_params=pltpu.CompilerParams(
            collective_id=0, has_side_effects=True, vmem_limit_bytes=VMEM_LIMIT
        ),
    )(
        features, grad_out, w_qkv, w_out, kept_slot, kept_count,
        jnp.transpose(fetch_slots, (2, 0, 1)),
    )
    return pl.pallas_call(
        copy_kernel, out_shape=out_shape, in_specs=[near, near], out_specs=[near, near]
    )(*results)


def solution(mesh):
    rows = P(("cluster", "head"), None)
    in_specs = (rows, rows, P(), P(), P("cluster", None), P("cluster"), P())
    return jax.shard_map(
        shards, mesh=mesh, in_specs=in_specs, out_specs=(rows, rows), check_vma=False
    )
```
